512 devices in a mesh: sub: 64 (over z, x), grp: 8 (over y, core).
Axes of the slice: x: 4, y: 4, z: 16, core: 2. Of those that a mesh axis runs over, the one named last changes fastest.
Arguments:
- schur: float32 [64, 8, 1024, 1024], P('sub', 'grp'), may hold values from -0.5 to 13, as said below
- loads: float32 [64, 8, 64, 1024], P('sub', 'grp'), may hold values from -30 to 30
- block_map: int32 [64, 8, 8], P('sub', 'grp'), may hold values from 0 to 7, each once within a row
- primal_map: int32 [64, 8, 8], P('sub', 'grp'), may hold values from 0 to 31
- disk_mask: int32 [64, 8, 1024], P('sub', 'grp'), may hold values 0 or 1
Outputs:
- solution: float32 [64, 8, 64, 1024], P('sub', 'grp')
- residual: float32 [64, 8, 64, 1024], P('sub', 'grp')
The draws below stay inside these ranges and needn't reach their ends.
Inputs may be any that keep to these rules, and one draw needn't show every extreme that they name: `schur`: each subdomain's Schur complement is symmetric with a strictly dominant positive diagonal.
All inputs are finite; a program needn't handle non-finite values. No bound on the sum of `disk_mask` on one device may be relied on, other than what follows from the above.
Results may differ from the reference program's by a relative error of at most 0.0003.
Values sent between devices are 32-bit elements; how exact they have to be, the bound alone decides.
A program may use at most 128 MiB of HBM per device.

```python
import math
import jax
import jax.numpy as jnp
from jax import lax

M = 1024
NRHS = 64
ITERS = 2
C = 32
N_SUB = 64
N_GRP = 8


def draw_schur(key, part):
    key = jax.random.fold_in(key, 11)
    key_off, key_diag, key_scale = jax.random.split(key, 3)
    drawn_ints = jax.random.randint(key_off, (N_SUB, N_GRP, M, M), 8192, 16384, dtype=jnp.int32)
    paired_ints = (drawn_ints + jnp.swapaxes(drawn_ints, 2, 3)) // 2
    places = jnp.arange(M, dtype=jnp.int32)
    distance = jnp.abs(places[:, None] - places[None, :])
    outside = (distance > 0).astype(jnp.int32)
    coupling = paired_ints // (1 + distance) * outside
    row_total = jnp.sum(coupling, axis=3)
    identity = jnp.eye(M, dtype=jnp.float32)
    margin = jnp.exp(jax.random.uniform(key_diag, (N_SUB, N_GRP, M), jnp.float32, math.log(0.01), math.log(0.05)))
    diagonal = row_total.astype(jnp.float32) / 32768.0 * (1.0 + margin)
    off_diag = -coupling.astype(jnp.float32) / 32768.0
    scales = jnp.exp(jax.random.uniform(key_scale, (N_SUB, N_GRP, 1, 1), jnp.float32, math.log(0.5), math.log(2.0)))
    matrix = off_diag + identity * diagonal[..., None]
    return matrix * scales


def draw_loads(key, part):
    key = jax.random.fold_in(key, 23)
    key_base, key_scale = jax.random.split(key)
    rising = jnp.exp(math.log(3.0) * jnp.arange(N_SUB, dtype=jnp.float32) / max(N_SUB - 1, 1))
    base = jax.random.normal(key_base, (N_SUB, N_GRP, NRHS, M), jnp.float32)
    scales = jnp.exp(jax.random.uniform(key_scale, (N_SUB, N_GRP, 1, 1), jnp.float32, math.log(0.7), math.log(1.4)))
    return base * rising[:, None, None, None] * scales


def touch_ends(values, rng, smallest, top_value):
    longest = values.shape.index(max(values.shape))
    spots = []
    for shift in (0, 1):
        where = [jax.random.randint(jax.random.fold_in(rng, axis), (), 0, length) for axis, length in enumerate(values.shape)]
        where[longest] = (where[longest] + shift) % values.shape[longest]
        spots.append(tuple(where))
    return values.at[spots[0]].set(smallest).at[spots[1]].set(top_value)


def setup_inputs(seed: int = 0) -> dict:
    streams_of = jax.random.split(jax.random.key(seed), 6)
    return {
        "schur": draw_schur(jax.random.fold_in(streams_of[5], 71), 0),
        "loads": draw_loads(jax.random.fold_in(streams_of[5], 71), 0),
        "block_map": jax.vmap(lambda own: jax.random.permutation(own, 8))(jax.random.split(streams_of[2], N_SUB * N_GRP)).reshape((N_SUB, N_GRP, 8)).astype(jnp.int32),
        "primal_map": touch_ends(jax.random.randint(streams_of[3], (N_SUB, N_GRP, 8), 0, C), jax.random.fold_in(streams_of[3], 1), 0, C - 1).astype(jnp.int32),
        "disk_mask": touch_ends((jax.random.randint(streams_of[4], (N_SUB, N_GRP, M), 0, 8) < 1).astype(jnp.int32), jax.random.fold_in(streams_of[4], 1), 0, 1),
    }


highest = lax.Precision.HIGHEST
disk_penalty = 0.1

def one_hot(indices, count):
    return (indices[..., None] == jnp.arange(count, dtype=jnp.int32)).astype(jnp.float32)

def chol_apply(factor, values):
    partial_sol = lax.linalg.triangular_solve(factor, values, left_side=False, lower=True, transpose_a=True)
    return lax.linalg.triangular_solve(factor, partial_sol, left_side=False, lower=True)

def reference(schur, loads, block_map, primal_map, disk_mask):
    domains = N_SUB * N_GRP
    block_width = M // 8
    half_size = M // 2
    root = math.sqrt(block_width)
    flattened = schur.reshape(domains, M, M)
    penalty = disk_penalty * disk_mask.reshape(domains, M).astype(jnp.float32)

    def prepare(pair):
        matrix, extra_diag = pair
        shifted = matrix + jnp.diag(extra_diag)
        sums = shifted.reshape(8, block_width, 8, block_width).sum(axis=(1, 3)) / block_width
        return (jnp.linalg.cholesky(shifted), sums)
    factors, block_sums = lax.map(prepare, (flattened, penalty))
    placing = one_hot(block_map.reshape(domains, 8), 8).reshape(domains, 8, 2, 4)
    primal = one_hot(primal_map.reshape(domains, 8), C)
    local_coarse = jnp.einsum('sjc,sjk,skd->scd', primal, block_sums, primal, precision=highest)
    grouped = local_coarse.reshape(N_SUB, N_GRP, C, C).sum(axis=1)
    coarse_factor = jnp.linalg.cholesky(grouped + jnp.eye(C, dtype=jnp.float32))

    def to_local(face_vals):
        blocks = face_vals.reshape(domains, 2, NRHS, 4, block_width)
        return jnp.einsum('shrqb,sjhq->srjb', blocks, placing, precision=highest).reshape(domains, NRHS, M)

    def to_faces(local_vals):
        blocks = local_vals.reshape(domains, NRHS, 8, block_width)
        return jnp.einsum('srjb,sjhq->shrqb', blocks, placing, precision=highest).reshape(domains, 2, NRHS, half_size)

    def assemble(face_vals):
        grid = face_vals.reshape(N_SUB, N_GRP, 2, NRHS, half_size)
        first_vec = grid[:, :, 0] + jnp.roll(grid[:, :, 1], 1, axis=0)
        second_vec = grid[:, :, 1] + jnp.roll(grid[:, :, 0], -1, axis=0)
        return jnp.stack([first_vec, second_vec], axis=2).reshape(domains, 2, NRHS, half_size)

    def operate(face_vals):
        local_vals = to_local(face_vals)
        product = jnp.einsum('srm,smn->srn', local_vals, flattened, precision=highest) + penalty[:, None, :] * local_vals
        return assemble(to_faces(product))

    def precondition(face_vals):
        weighted = 0.5 * to_local(face_vals)
        solved = chol_apply(factors, weighted)
        averages = weighted.reshape(domains, NRHS, 8, block_width).sum(axis=3) / root
        contrib = jnp.einsum('srj,sjc->src', averages, primal, precision=highest)
        coarse_rhs = contrib.reshape(N_SUB, N_GRP, NRHS, C).sum(axis=1)
        amounts = chol_apply(coarse_factor, coarse_rhs)
        amounts = jnp.broadcast_to(amounts[:, None], (N_SUB, N_GRP, NRHS, C)).reshape(domains, NRHS, C)
        spread = jnp.einsum('src,sjc->srj', amounts, primal, precision=highest) / root
        correction = jnp.broadcast_to(spread[..., None], (domains, NRHS, 8, block_width)).reshape(domains, NRHS, M)
        return assemble(to_faces(0.5 * (solved + correction)))

    def inner(first_vec, second_vec):
        return lax.optimization_barrier(jnp.sum(first_vec[:, 1] * second_vec[:, 1], axis=(0, 2)))
    right_side = assemble(to_faces(loads.reshape(domains, NRHS, M)))
    solution = jnp.zeros_like(right_side)
    residual = right_side
    precond = precondition(residual)
    direction = precond
    energy = inner(residual, precond)
    for iteration in range(ITERS):
        image = operate(direction)
        alpha = (energy / inner(direction, image))[None, None, :, None]
        solution = solution + alpha * direction
        residual = residual - alpha * image
        if iteration + 1 < ITERS:
            precond = precondition(residual)
            fresh = inner(residual, precond)
            direction = precond + (fresh / energy)[None, None, :, None] * direction
            energy = fresh

    def to_output(face_vals):
        return jnp.transpose(face_vals, (0, 2, 1, 3)).reshape(N_SUB, N_GRP, NRHS, M)
    return (to_output(solution), to_output(residual))
```

```python
import jax
import jax.numpy as jnp
from jax import lax
from jax.experimental import pallas as pl
from jax.experimental.pallas import tpu as pltpu
from jax.sharding import PartitionSpec as P

F32 = jnp.float32
BF16 = jnp.bfloat16
HI = lax.Precision.HIGHEST
MESH = pl.DeviceIdType.MESH
M = 1024
R = 64
BW = 128
NB = 8
C = 32
X_DIM = 4
ROOT = BW ** 0.5
MIB = 1 << 20


def vmem():
    return pl.BlockSpec(memory_space=pltpu.VMEM)


def smem():
    return pl.BlockSpec(memory_space=pltpu.SMEM)


def split(value):
    high = value.astype(BF16)
    low = (value - high.astype(F32)).astype(BF16)
    return high, low


def dot(a, b):
    return jnp.dot(a, b, preferred_element_type=F32)


def dot_hi(a, b, dims):
    return lax.dot_general(a, b, (dims, ((), ())), precision=HI, preferred_element_type=F32)


def spread(v):
    return jnp.broadcast_to(v, (8, BW))


def recip(a):
    r = pltpu.reciprocal(a, approx=True)
    r = r * (2.0 - a * r)
    return r * (2.0 - a * r)


def small_mm(a, b):
    out = []
    for i in range(len(a)):
        row = []
        for j in range(len(b[0])):
            t = a[i][0] * b[0][j]
            for l in range(1, len(b)):
                t = t + a[i][l] * b[l][j]
            row.append(t)
        out.append(row)
    return out


def small_inverse(d):
    n = len(d)
    if n == 2:
        a, b, e = d[0][0], d[0][1], d[1][1]
        r = recip(a * e - b * b)
        o = -(b * r)
        return [[e * r, o], [o, a * r]]
    h = n // 2
    a = small_inverse([row[:h] for row in d[:h]])
    b = [row[h:] for row in d[:h]]
    t = small_mm(a, b)
    s = [[None] * h for _ in range(h)]
    for i in range(h):
        for j in range(i, h):
            u = b[0][i] * t[0][j]
            for l in range(1, h):
                u = u + b[l][i] * t[l][j]
            s[i][j] = d[h + i][h + j] - u
            s[j][i] = s[i][j]
    s = small_inverse(s)
    ts = small_mm(t, s)
    r = [[None] * n for _ in range(n)]
    for i in range(h):
        for j in range(h):
            r[h + i][h + j] = s[i][j]
            r[i][h + j] = -ts[i][j]
            r[h + j][i] = r[i][h + j]
    for i in range(h):
        for j in range(i, h):
            u = a[i][j]
            for l in range(h):
                u = u + ts[i][l] * t[j][l]
            r[i][j] = u
            r[j][i] = u
    return r


def dense_inverse(x, n):
    groups = n // 8
    xs = [x[8 * i : 8 * i + 8, :] for i in range(groups)]
    lane = lax.broadcasted_iota(jnp.int32, (8, BW), 1)
    sub = lax.broadcasted_iota(jnp.int32, (8, BW), 0)
    for q in range(groups):
        k = 8 * q
        rows = [spread(xs[q][j : j + 1, :]) for j in range(8)]
        d = [[None] * 8 for _ in range(8)]
        for i in range(8):
            for j in range(i, 8):
                d[i][j] = spread(rows[i][:, k + j : k + j + 1])
                d[j][i] = d[i][j]
        cols = [[spread(xs[i][:, k + j : k + j + 1]) for j in range(8)] for i in range(groups)]
        r = small_inverse(d)
        p = []
        for i in range(8):
            u = r[i][0] * rows[0]
            for j in range(1, 8):
                u = u + r[i][j] * rows[j]
            for j in range(8):
                u = jnp.where(lane == k + j, r[i][j], u)
            p.append(u)
        pivots = (lane >= k) & (lane < k + 8)
        new = []
        for i in range(groups):
            if i == q:
                y = p[0]
                for j in range(1, 8):
                    y = jnp.where(sub == j, p[j], y)
            else:
                y = jnp.where(pivots, 0.0, xs[i])
                for j in range(8):
                    y = y - cols[i][j] * p[j]
            new.append(y)
        xs = new
    return jnp.concatenate(xs, 0)


def face_sources(bm_ref):
    places = [bm_ref[0, j] for j in range(NB)]
    out = []
    for f in range(NB):
        where = jnp.int32(0)
        for j in range(NB):
            where = where + jnp.where(places[j] == f, jnp.int32(j), jnp.int32(0))
        out.append(where)
    return out


def prepare_kernel(bm_ref, pm_ref, schur_ref, loads_ref, mask_ref, face_ref, tile_ref, sums):
    source = face_sources(bm_ref)
    lanes = lax.broadcasted_iota(jnp.int32, (1, M), 1) // BW
    penalty = 0.1 * mask_ref[...].astype(F32)
    sub = lax.broadcasted_iota(jnp.int32, (8, BW), 0)
    lane = lax.broadcasted_iota(jnp.int32, (8, BW), 1)
    primal = jnp.zeros((8, BW), F32)
    shifted = jnp.zeros((8, BW), F32)
    picks = []
    for f in range(NB):
        at = pl.multiple_of(source[f] * BW, BW)
        face_ref[:, f * BW : (f + 1) * BW] = loads_ref[:, pl.ds(at, BW)]
        mine = lanes == source[f]
        row = jnp.sum(schur_ref[pl.ds(at, BW), :], axis=0, keepdims=True)
        sums[f : f + 1, :] = row + jnp.where(mine, penalty, 0.0)
        picks.append(mine.astype(F32))
        coarse = pm_ref[0, source[f]]
        primal = jnp.where((sub == f) & (lane == coarse), 1.0, primal)
        shifted = jnp.where((sub == f) & (lane == coarse + C), 1.0, shifted)
    pick = jnp.concatenate(picks, 0)
    block_sums = dot_hi(sums[...], pick, ((1,), (1,))) / BW
    tile_ref[...] = dot_hi(block_sums, primal, ((1,), (0,))) + shifted


def prepare(block_map, primal_map, schur, loads, mask):
    return pl.pallas_call(
        prepare_kernel,
        out_shape=(
            jax.ShapeDtypeStruct((R, M), F32),
            jax.ShapeDtypeStruct((8, BW), F32),
        ),
        in_specs=[smem(), smem(), vmem(), vmem(), vmem()],
        out_specs=(vmem(), vmem()),
        scratch_shapes=[pltpu.VMEM((8, M), F32)],
        compiler_params=pltpu.CompilerParams(vmem_limit_bytes=16 * MIB),
        name="prepare",
    )(block_map, primal_map, schur, loads, mask)


def invert_kernel(
    bm_ref, schur_ref, mask_ref, ah_ref, al_ref, xh_ref, xl_ref, x, col, rhs_h, rhs_l, panel
):
    source = face_sources(bm_ref)
    eye = lax.broadcasted_iota(jnp.int32, (BW, BW), 0) == lax.broadcasted_iota(
        jnp.int32, (BW, BW), 1
    )
    for f in range(NB):
        row_at = pl.multiple_of(source[f] * BW, BW)
        for h in range(NB):
            col_at = pl.multiple_of(source[h] * BW, BW)
            block = schur_ref[pl.ds(row_at, BW), pl.ds(col_at, BW)]
            if f == h:
                penalty = 0.1 * mask_ref[:, pl.ds(col_at, BW)].astype(F32)
                block = block + jnp.where(eye, penalty, 0.0)
            x[f * BW : (f + 1) * BW, h * BW : (h + 1) * BW] = block
            high, low = split(block)
            ah_ref[f * BW : (f + 1) * BW, h * BW : (h + 1) * BW] = high
            al_ref[f * BW : (f + 1) * BW, h * BW : (h + 1) * BW] = low

    def step(k, carry):
        at = pl.multiple_of(k * BW, BW)
        here = pl.ds(at, BW)
        inverse = dense_inverse(x[here, here], BW)
        inv_h, inv_l = split(inverse)
        row_h, row_l = split(x[here, :])
        both = jnp.concatenate([inv_h, inv_l], 1)
        p = dot(both, jnp.concatenate([row_h, row_h], 0)) + dot(
            both, jnp.concatenate([row_l, row_l], 0)
        )
        panel[...] = p
        panel[:, here] = inverse
        p_h, p_l = split(panel[...])
        rhs_h[0:BW, :] = p_h
        rhs_h[BW:, :] = p_h
        rhs_l[0:BW, :] = p_l
        rhs_l[BW:, :] = p_l
        col_h, col_l = split(x[:, here])
        col[:, 0:BW] = col_h
        col[:, BW:] = col_l
        x[:, here] = jnp.zeros((M, BW), F32)
        for n in range(4):
            cols = slice(n * 256, (n + 1) * 256)
            x[:, cols] = x[:, cols] - (
                dot(col[...], rhs_h[:, cols]) + dot(col[...], rhs_l[:, cols])
            )
        x[here, :] = panel[...]
        return carry

    lax.fori_loop(0, NB, step, 0)
    for f in range(NB):
        rows = slice(f * BW, (f + 1) * BW)
        high, low = split(x[rows, :])
        xh_ref[rows, :] = high
        xl_ref[rows, :] = low


def invert(block_map, schur, mask):
    big = jax.ShapeDtypeStruct((M, M), BF16)
    return pl.pallas_call(
        invert_kernel,
        out_shape=(big, big, big, big),
        in_specs=[smem(), vmem(), vmem()],
        out_specs=(vmem(), vmem(), vmem(), vmem()),
        scratch_shapes=[
            pltpu.VMEM((M, M), F32),
            pltpu.VMEM((M, 2 * BW), BF16),
            pltpu.VMEM((2 * BW, M), BF16),
            pltpu.VMEM((2 * BW, M), BF16),
            pltpu.VMEM((BW, M), F32),
        ],
        compiler_params=pltpu.CompilerParams(vmem_limit_bytes=40 * MIB),
        cost_estimate=pl.CostEstimate(
            flops=20_000_000_000, bytes_accessed=12 * MIB, transcendentals=0
        ),
        name="invert",
    )(block_map, schur, mask)


def product(value, high_ref, low_ref):
    high, low = split(value)
    both = dot(jnp.concatenate([high, low], 0), high_ref[...])
    return both[:R] + both[R:] + dot(high, low_ref[...])


def iterate_kernel(
    loads_ref, low_ref, high_ref, tiles_ref, ah_ref, al_ref, xh_ref, xl_ref,
    sol_ref, res_ref,
    face_out, face_in, avg, sum_g, sum_x, sum_z,
    face_send, face_recv, avg_send, avg_recv, g_send, g_recv, x_send, x_recv, z_send, z_recv,
):
    s = lax.axis_index("sub")
    g = lax.axis_index("grp")
    n_sub = lax.axis_size("sub")
    n_grp = lax.axis_size("grp")
    n_z = n_sub // X_DIM
    xi = lax.rem(s, X_DIM)
    zi = s // X_DIM
    left = lax.rem(s + n_sub - 1, n_sub)
    right = lax.rem(s + 1, n_sub)

    def grp_peer(d):
        return (s, lax.rem(g + d, n_grp))

    def x_peer(d):
        return (zi * X_DIM + lax.rem(xi + d, X_DIM), g)

    def z_peer(d):
        return (lax.rem(zi + d, n_z) * X_DIM + xi, g)

    partners = [(left, g), (right, g)]
    partners += [grp_peer(d) for d in range(1, n_grp)]
    partners += [x_peer(d) for d in range(1, X_DIM)]
    partners += [z_peer(d) for d in range(1, n_z)]
    barrier = pltpu.get_barrier_semaphore()
    for partner in partners:
        pl.semaphore_signal(barrier, inc=1, device_id=partner, device_id_type=MESH)

    started = []

    def gather_start(buf, e, send, recv, peer, count, mine):
        for d in range(1, count):
            copy = pltpu.make_async_remote_copy(
                src_ref=buf.at[e, mine], dst_ref=buf.at[e, mine],
                send_sem=send.at[e, d], recv_sem=recv.at[e, mine],
                device_id=peer(d), device_id_type=MESH,
            )
            copy.start()
            started.append(copy)

    def gather_wait(buf, e, send, recv, peer, count, mine):
        for d in range(1, count):
            other = lax.rem(mine + d, count)
            pltpu.make_async_remote_copy(
                src_ref=buf.at[e, other], dst_ref=buf.at[e, other],
                send_sem=send.at[e, d], recv_sem=recv.at[e, other],
                device_id=peer(d), device_id_type=MESH,
            ).wait_recv()

    stages = {
        "avg": (avg, avg_send, avg_recv, grp_peer, n_grp, g),
        "g": (sum_g, g_send, g_recv, grp_peer, n_grp, g),
        "x": (sum_x, x_send, x_recv, x_peer, X_DIM, xi),
        "z": (sum_z, z_send, z_recv, z_peer, n_z, zi),
    }

    def begin(stage, e, tile):
        buf, send, recv, peer, count, mine = stages[stage]
        buf[e, mine] = tile
        gather_start(buf, e, send, recv, peer, count, mine)

    def end(stage, e):
        buf, send, recv, peer, count, mine = stages[stage]
        gather_wait(buf, e, send, recv, peer, count, mine)
        return buf

    def total(stage, e):
        buf = end(stage, e)
        out = buf[e, 0]
        for d in range(1, buf.shape[1]):
            out = out + buf[e, d]
        return out

    def exchange_start(e, value):
        face_out[e, 0] = value[:, : M // 2]
        face_out[e, 1] = value[:, M // 2 :]
        for side, target in ((0, left), (1, right)):
            copy = pltpu.make_async_remote_copy(
                src_ref=face_out.at[e, side], dst_ref=face_in.at[e, 1 - side],
                send_sem=face_send.at[e, side], recv_sem=face_recv.at[e, 1 - side],
                device_id=(target, g), device_id_type=MESH,
            )
            copy.start()
            started.append(copy)

    def exchange_end(e):
        for side, target in ((0, left), (1, right)):
            pltpu.make_async_remote_copy(
                src_ref=face_out.at[e, side], dst_ref=face_in.at[e, 1 - side],
                send_sem=face_send.at[e, side], recv_sem=face_recv.at[e, 1 - side],
                device_id=(target, g), device_id_type=MESH,
            ).wait_recv()
        first = face_out[e, 0] + face_in[e, 0]
        second = face_out[e, 1] + face_in[e, 1]
        return jnp.concatenate([first, second], 1)

    blocks = (
        lax.broadcasted_iota(jnp.int32, (8, M), 1) // BW
        == lax.broadcasted_iota(jnp.int32, (8, M), 0)
    ).astype(F32)
    sub = lax.broadcasted_iota(jnp.int32, (8, BW), 0)
    ones = jnp.ones((8, M), F32)
    pad = jnp.zeros((8, BW - R), F32)

    def averages(w):
        t = dot_hi(blocks, w, ((1,), (1,))) * (1.0 / ROOT)
        return jnp.concatenate([t, pad], 1)

    def sums_of(u, v):
        t = dot_hi(ones, u * v, ((1,), (1,)))
        return jnp.concatenate([t, pad], 1)

    def per_row(line):
        tile = jnp.where(sub == 0, jnp.broadcast_to(line, (8, BW)), 0.0)
        wide = dot_hi(tile, jnp.ones((8, BW), F32), ((0,), (0,)))[:R]
        return jnp.concatenate([wide] * NB, 1)

    right_side = loads_ref[...] + jnp.concatenate([low_ref[...], high_ref[...]], 1)
    weighted = 0.5 * right_side
    tile = averages(weighted)
    pl.semaphore_wait(barrier, len(partners))
    begin("avg", 0, tile)

    contributions = tiles_ref[...].reshape(n_grp * 8, BW)
    primal_all = contributions[:, C : 2 * C]
    local_all = contributions[:, :C]
    coarse = dot_hi(primal_all, local_all, ((0,), (0,)))
    coarse = coarse + (
        lax.broadcasted_iota(jnp.int32, (C, C), 0) == lax.broadcasted_iota(jnp.int32, (C, C), 1)
    ).astype(F32)
    coarse_inverse = dense_inverse(
        jnp.concatenate([coarse, jnp.zeros((C, BW - C), F32)], 1), C
    )[:, :C]
    primal = tiles_ref[g][:, C : 2 * C]
    weights = dot_hi(dot_hi(primal, coarse_inverse, ((1,), (0,))), primal_all, ((1,), (1,)))

    def correction(e):
        gathered = end("avg", e)[e].reshape(n_grp * 8, BW)
        amounts = dot_hi(weights, gathered, ((1,), (0,))) * (1.0 / ROOT)
        return dot_hi(amounts[:, :R], blocks, ((0,), (0,)))

    solved = product(weighted, xh_ref, xl_ref)
    local_z = 0.5 * (solved + correction(0))
    exchange_start(0, local_z)
    rz = sums_of(right_side, local_z)
    z = exchange_end(0)

    prod = product(z, ah_ref, al_ref)
    exchange_start(1, prod)
    dp = sums_of(z, prod)
    begin("g", 0, jnp.where(sub == 0, rz, dp))
    image = exchange_end(1)

    half = 0.5 * image
    begin("avg", 1, averages(half))
    begin("x", 0, total("g", 0))
    solved_q = product(half, xh_ref, xl_ref)
    local_q = 0.5 * (solved_q + correction(1))
    exchange_start(2, local_q)
    begin("z", 0, total("x", 0))
    first = total("z", 0)
    rz0 = first[0:1]
    dp0 = first[1:2]
    alpha0 = rz0 / jnp.where(lax.broadcasted_iota(jnp.int32, (1, BW), 1) < R, dp0, 1.0)
    alpha0_rows = per_row(alpha0)
    residual = right_side - alpha0_rows * image
    rz = sums_of(residual, local_z - alpha0_rows * local_q)
    z1 = z - alpha0_rows * exchange_end(2)

    prod1 = product(z1, ah_ref, al_ref)
    exchange_start(3, prod1)
    zz = sums_of(z1, prod1)
    zd = sums_of(z1, prod)
    begin("g", 1, jnp.where(sub == 0, rz, jnp.where(sub == 1, zz, zd)))
    begin("x", 1, total("g", 1))
    image1 = exchange_end(3)
    begin("z", 1, total("x", 1))
    last = total("z", 1)
    valid = lax.broadcasted_iota(jnp.int32, (1, BW), 1) < R
    rz1 = last[0:1]
    beta = rz1 / jnp.where(valid, rz0, 1.0)
    energy = last[1:2] + 2.0 * beta * last[2:3] + beta * beta * dp0
    alpha1 = rz1 / jnp.where(valid, energy, 1.0)
    alpha1_rows = per_row(alpha1)
    beta_rows = per_row(beta)
    sol_ref[...] = alpha0_rows * z + alpha1_rows * (z1 + beta_rows * z)
    res_ref[...] = residual - alpha1_rows * (image1 + beta_rows * image)
    for copy in started:
        copy.wait_send()


def iterate(n_grp, n_sub, *args):
    n_z = n_sub // X_DIM
    out = jax.ShapeDtypeStruct((R, M), F32)
    dma = pltpu.SemaphoreType.DMA
    return pl.pallas_call(
        iterate_kernel,
        out_shape=(out, out),
        in_specs=[vmem()] * 8,
        out_specs=(vmem(), vmem()),
        scratch_shapes=[
            pltpu.VMEM((4, 2, R, M // 2), F32),
            pltpu.VMEM((4, 2, R, M // 2), F32),
            pltpu.VMEM((2, n_grp, 8, BW), F32),
            pltpu.VMEM((2, n_grp, 8, BW), F32),
            pltpu.VMEM((2, X_DIM, 8, BW), F32),
            pltpu.VMEM((2, n_z, 8, BW), F32),
            dma((4, 2)),
            dma((4, 2)),
            dma((2, n_grp)),
            dma((2, n_grp)),
            dma((2, n_grp)),
            dma((2, n_grp)),
            dma((2, X_DIM)),
            dma((2, X_DIM)),
            dma((2, n_z)),
            dma((2, n_z)),
        ],
        compiler_params=pltpu.CompilerParams(
            collective_id=0, has_side_effects=True, vmem_limit_bytes=40 * MIB
        ),
        cost_estimate=pl.CostEstimate(
            flops=2_000_000_000, bytes_accessed=10 * MIB, transcendentals=0
        ),
        name="iterate",
    )(*args)


def body(schur, loads, block_map, primal_map, disk_mask):
    n_sub = lax.axis_size("sub")
    n_grp = lax.axis_size("grp")
    block_map = block_map[0]
    matrix = schur[0, 0]
    mask = disk_mask[0]
    face, tile = prepare(block_map, primal_map[0], matrix, loads[0, 0], mask)
    forward = [(i, (i + 1) % n_sub) for i in range(n_sub)]
    backward = [(i, (i - 1) % n_sub) for i in range(n_sub)]
    from_left = lax.ppermute(face[:, M // 2 :], "sub", forward)
    from_right = lax.ppermute(face[:, : M // 2], "sub", backward)
    tiles = lax.all_gather(tile, "grp")
    a_high, a_low, x_high, x_low = invert(block_map, matrix, mask)
    sol, res = iterate(
        n_grp, n_sub, face, from_left, from_right, tiles, a_high, a_low, x_high, x_low
    )
    return sol[None, None], res[None, None]


def solution(mesh):
    in_specs = (
        P("sub", "grp", None, None),
        P("sub", "grp", None, None),
        P("sub", "grp", None),
        P("sub", "grp", None),
        P("sub", "grp", None),
    )
    out_specs = (P("sub", "grp", None, None), P("sub", "grp", None, None))
    return jax.shard_map(body, mesh=mesh, in_specs=in_specs, out_specs=out_specs, check_vma=False)
```

```python
import jax
import jax.numpy as jnp
from jax import lax
from jax.experimental import pallas as pl
from jax.experimental.pallas import tpu as pltpu
from jax.sharding import PartitionSpec as P

F32 = jnp.float32
BF16 = jnp.bfloat16
HI = lax.Precision.HIGHEST
MESH = pl.DeviceIdType.MESH
M = 1024
R = 64
BW = 128
NB = 8
C = 32
X_DIM = 4
ROOT = BW ** 0.5
MIB = 1 << 20


def vmem():
    return pl.BlockSpec(memory_space=pltpu.VMEM)


def smem():
    return pl.BlockSpec(memory_space=pltpu.SMEM)


def split(value):
    high = value.astype(BF16)
    low = (value - high.astype(F32)).astype(BF16)
    return high, low


def dot(a, b):
    return jnp.dot(a, b, preferred_element_type=F32)


def dot_hi(a, b, dims):
    return lax.dot_general(a, b, (dims, ((), ())), precision=HI, preferred_element_type=F32)


def spread(v):
    return jnp.broadcast_to(v, (8, BW))


def recip(a):
    r = pltpu.reciprocal(a, approx=True)
    return r * (2.0 - a * r)


def small_mm(a, b):
    out = []
    for i in range(len(a)):
        row = []
        for j in range(len(b[0])):
            t = a[i][0] * b[0][j]
            for l in range(1, len(b)):
                t = t + a[i][l] * b[l][j]
            row.append(t)
        out.append(row)
    return out


def small_inverse(d):
    n = len(d)
    if n == 2:
        a, b, e = d[0][0], d[0][1], d[1][1]
        r = recip(a * e - b * b)
        o = -(b * r)
        return [[e * r, o], [o, a * r]]
    h = n // 2
    a = small_inverse([row[:h] for row in d[:h]])
    b = [row[h:] for row in d[:h]]
    t = small_mm(a, b)
    s = [[None] * h for _ in range(h)]
    for i in range(h):
        for j in range(i, h):
            u = b[0][i] * t[0][j]
            for l in range(1, h):
                u = u + b[l][i] * t[l][j]
            s[i][j] = d[h + i][h + j] - u
            s[j][i] = s[i][j]
    s = small_inverse(s)
    ts = small_mm(t, s)
    r = [[None] * n for _ in range(n)]
    for i in range(h):
        for j in range(h):
            r[h + i][h + j] = s[i][j]
            r[i][h + j] = -ts[i][j]
            r[h + j][i] = r[i][h + j]
    for i in range(h):
        for j in range(i, h):
            u = a[i][j]
            for l in range(h):
                u = u + ts[i][l] * t[j][l]
            r[i][j] = u
            r[j][i] = u
    return r


def dense_inverse(x, n, beside=()):
    beside = list(beside)
    groups = n // 8
    xs = [x[8 * i : 8 * i + 8, :] for i in range(groups)]
    lane = lax.broadcasted_iota(jnp.int32, (8, BW), 1)
    sub = lax.broadcasted_iota(jnp.int32, (8, BW), 0)
    for q in range(groups):
        k = 8 * q
        rows = [spread(xs[q][j : j + 1, :]) for j in range(8)]
        d = [[None] * 8 for _ in range(8)]
        for i in range(8):
            for j in range(i, 8):
                d[i][j] = spread(rows[i][:, k + j : k + j + 1])
                d[j][i] = d[i][j]
        cols = [[spread(xs[i][:, k + j : k + j + 1]) for j in range(8)] for i in range(groups)]
        r = small_inverse(d)
        p = []
        for i in range(8):
            u = r[i][0] * rows[0]
            for j in range(1, 8):
                u = u + r[i][j] * rows[j]
            for j in range(8):
                u = jnp.where(lane == k + j, r[i][j], u)
            p.append(u)
        pivots = (lane >= k) & (lane < k + 8)
        new = []
        for i in range(groups):
            if i == q:
                y = p[0]
                for j in range(1, 8):
                    y = jnp.where(sub == j, p[j], y)
            else:
                y = jnp.where(pivots, 0.0, xs[i])
                for j in range(8):
                    y = y - cols[i][j] * p[j]
            new.append(y)
        xs = new
        if beside:
            beside.pop(0)()
    for work in beside:
        work()
    return jnp.concatenate(xs, 0)


def face_sources(bm_ref):
    places = [bm_ref[0, j] for j in range(NB)]
    out = []
    for f in range(NB):
        where = jnp.int32(0)
        for j in range(NB):
            where = where + jnp.where(places[j] == f, jnp.int32(j), jnp.int32(0))
        out.append(where)
    return out


def prepare_kernel(bm_ref, pm_ref, schur_ref, loads_ref, mask_ref, face_ref, tile_ref, sums):
    source = face_sources(bm_ref)
    lanes = lax.broadcasted_iota(jnp.int32, (1, M), 1) // BW
    penalty = 0.1 * mask_ref[...].astype(F32)
    sub = lax.broadcasted_iota(jnp.int32, (8, BW), 0)
    lane = lax.broadcasted_iota(jnp.int32, (8, BW), 1)
    primal = jnp.zeros((8, BW), F32)
    shifted = jnp.zeros((8, BW), F32)
    picks = []
    for f in range(NB):
        at = pl.multiple_of(source[f] * BW, BW)
        face_ref[:, f * BW : (f + 1) * BW] = loads_ref[:, pl.ds(at, BW)]
        mine = lanes == source[f]
        row = jnp.sum(schur_ref[pl.ds(at, BW), :], axis=0, keepdims=True)
        sums[f : f + 1, :] = row + jnp.where(mine, penalty, 0.0)
        picks.append(mine.astype(F32))
        coarse = pm_ref[0, source[f]]
        primal = jnp.where((sub == f) & (lane == coarse), 1.0, primal)
        shifted = jnp.where((sub == f) & (lane == coarse + C), 1.0, shifted)
    pick = jnp.concatenate(picks, 0)
    block_sums = dot_hi(sums[...], pick, ((1,), (1,))) / BW
    tile_ref[...] = dot_hi(block_sums, primal, ((1,), (0,))) + shifted


def prepare(block_map, primal_map, schur, loads, mask):
    return pl.pallas_call(
        prepare_kernel,
        out_shape=(
            jax.ShapeDtypeStruct((R, M), F32),
            jax.ShapeDtypeStruct((8, BW), F32),
        ),
        in_specs=[smem(), smem(), vmem(), vmem(), vmem()],
        out_specs=(vmem(), vmem()),
        scratch_shapes=[pltpu.VMEM((8, M), F32)],
        compiler_params=pltpu.CompilerParams(vmem_limit_bytes=16 * MIB),
        name="prepare",
    )(block_map, primal_map, schur, loads, mask)


def invert_kernel(
    bm_ref, schur_ref, mask_ref, ah_ref, al_ref, out_ref, col, last_ref,
    x, rhs, panel, pivot, inv,
):
    source = face_sources(bm_ref)
    eye = lax.broadcasted_iota(jnp.int32, (BW, BW), 0) == lax.broadcasted_iota(
        jnp.int32, (BW, BW), 1
    )
    for f in range(NB):
        row_at = pl.multiple_of(source[f] * BW, BW)
        for h in range(NB):
            col_at = pl.multiple_of(source[h] * BW, BW)
            block = schur_ref[pl.ds(row_at, BW), pl.ds(col_at, BW)]
            if f == h:
                penalty = 0.1 * mask_ref[:, pl.ds(col_at, BW)].astype(F32)
                block = block + jnp.where(eye, penalty, 0.0)
            x[f * BW : (f + 1) * BW, h * BW : (h + 1) * BW] = block
            high, low = split(block)
            ah_ref[f * BW : (f + 1) * BW, h * BW : (h + 1) * BW] = high
            al_ref[f * BW : (f + 1) * BW, h * BW : (h + 1) * BW] = low
    x[M:, :] = jnp.zeros((BW, M + BW), F32)
    x[:M, M:] = jnp.zeros((M, BW), F32)
    inv[...] = jnp.zeros((BW, BW), F32)
    pivot[...] = x[0:BW, 0:BW]

    def at(k):
        return pl.ds(pl.multiple_of(k * BW, BW), BW)

    def four(value, axis):
        high, low = split(value)
        parts = [high, low, high, low] if axis == 1 else [high, high, low, low]
        return jnp.concatenate(parts, axis)

    def rest(here):
        def rows():
            inverse = inv[...]
            panel[...] = dot(four(inverse, 1), four(x[here, :M], 0))
            col[...] = four(x[:M, here], 1)
            x[:, here] = jnp.zeros((M + BW, BW), F32)

        def finish():
            x[here, :M] = panel[...]
            x[here, here] = inv[...]

        def block(n):
            cols = slice(n * 256, (n + 1) * 256)

            def work():
                x[:M, cols] = x[:M, cols] - dot(col[...], rhs[:, cols])

            return work

        def sides():
            rhs[:, :M] = four(panel[...], 0)
            rhs[:, here] = four(inv[...], 0)

        return rows, sides, [block(n) for n in range(4)], finish

    def step(k, carry):
        last = at(lax.rem(k + NB, NB + 1))
        here = at(k)
        after = at(jnp.minimum(k + 1, NB - 1))
        rows, sides, blocks, finish = rest(last)
        rows()
        sides()

        def nothing():
            pass

        work = []
        for block in blocks:
            work += [block, nothing, nothing]
        inverse = dense_inverse(pivot[...], BW, work)
        finish()
        inv[...] = inverse
        p = dot(four(inverse, 1), four(x[here, after], 0))
        pivot[...] = x[after, after] - dot(four(x[after, here], 1), four(p, 0))
        return carry

    lax.fori_loop(0, NB, step, 0)
    rows, sides, blocks, finish = rest(at(NB - 1))
    rows()
    sides()
    finish()
    col[M - BW :, :] = jnp.zeros((BW, 4 * BW), BF16)
    last_ref[...] = rhs[:, :M]
    out_ref[...] = x[:M, :M]


def invert(block_map, schur, mask):
    big = jax.ShapeDtypeStruct((M, M), BF16)
    return pl.pallas_call(
        invert_kernel,
        out_shape=(
            big,
            big,
            jax.ShapeDtypeStruct((M, M), F32),
            jax.ShapeDtypeStruct((M, 4 * BW), BF16),
            jax.ShapeDtypeStruct((4 * BW, M), BF16),
        ),
        in_specs=[smem(), vmem(), vmem()],
        out_specs=(vmem(),) * 5,
        scratch_shapes=[
            pltpu.VMEM((M + BW, M + BW), F32),
            pltpu.VMEM((4 * BW, M + BW), BF16),
            pltpu.VMEM((BW, M), F32),
            pltpu.VMEM((BW, BW), F32),
            pltpu.VMEM((BW, BW), F32),
        ],
        compiler_params=pltpu.CompilerParams(vmem_limit_bytes=40 * MIB),
        cost_estimate=pl.CostEstimate(
            flops=20_000_000_000, bytes_accessed=12 * MIB, transcendentals=0
        ),
        name="invert",
    )(block_map, schur, mask)


def product(value, high_ref, low_ref):
    high, low = split(value)
    both = dot(jnp.concatenate([high, low], 0), high_ref[...])
    return both[:R] + both[R:] + dot(high, low_ref[...])


def iterate_kernel(
    loads_ref, tile_ref, ah_ref, al_ref, x_ref, col_ref, rhs_ref,
    sol_ref, res_ref,
    xh_ref, xl_ref, face_out, face_in, avg, sum_g, sum_x, sum_z,
    face_send, face_recv, avg_send, avg_recv, g_send, g_recv, x_send, x_recv, z_send, z_recv,
):
    s = lax.axis_index("sub")
    g = lax.axis_index("grp")
    n_sub = lax.axis_size("sub")
    n_grp = lax.axis_size("grp")
    n_z = n_sub // X_DIM
    xi = lax.rem(s, X_DIM)
    zi = s // X_DIM
    left = lax.rem(s + n_sub - 1, n_sub)
    right = lax.rem(s + 1, n_sub)

    def grp_peer(d):
        return (s, lax.rem(g + d, n_grp))

    def x_peer(d):
        return (zi * X_DIM + lax.rem(xi + d, X_DIM), g)

    def z_peer(d):
        return (lax.rem(zi + d, n_z) * X_DIM + xi, g)

    partners = [(left, g), (right, g)]
    partners += [grp_peer(d) for d in range(1, n_grp)]
    partners += [x_peer(d) for d in range(1, X_DIM)]
    partners += [z_peer(d) for d in range(1, n_z)]
    barrier = pltpu.get_barrier_semaphore()
    for partner in partners:
        pl.semaphore_signal(barrier, inc=1, device_id=partner, device_id_type=MESH)

    started = []

    def gather_start(buf, e, send, recv, peer, count, mine):
        for d in range(1, count):
            copy = pltpu.make_async_remote_copy(
                src_ref=buf.at[e, mine], dst_ref=buf.at[e, mine],
                send_sem=send.at[e, d], recv_sem=recv.at[e, mine],
                device_id=peer(d), device_id_type=MESH,
            )
            copy.start()
            started.append(copy)

    def gather_wait(buf, e, send, recv, peer, count, mine):
        for d in range(1, count):
            other = lax.rem(mine + d, count)
            pltpu.make_async_remote_copy(
                src_ref=buf.at[e, other], dst_ref=buf.at[e, other],
                send_sem=send.at[e, d], recv_sem=recv.at[e, other],
                device_id=peer(d), device_id_type=MESH,
            ).wait_recv()

    stages = {
        "avg": (avg, avg_send, avg_recv, grp_peer, n_grp, g),
        "g": (sum_g, g_send, g_recv, grp_peer, n_grp, g),
        "x": (sum_x, x_send, x_recv, x_peer, X_DIM, xi),
        "z": (sum_z, z_send, z_recv, z_peer, n_z, zi),
    }

    def begin(stage, e, tile):
        buf, send, recv, peer, count, mine = stages[stage]
        buf[e, mine] = tile
        gather_start(buf, e, send, recv, peer, count, mine)

    def end(stage, e):
        buf, send, recv, peer, count, mine = stages[stage]
        gather_wait(buf, e, send, recv, peer, count, mine)
        return buf

    def total(stage, e):
        buf = end(stage, e)
        out = buf[e, 0]
        for d in range(1, buf.shape[1]):
            out = out + buf[e, d]
        return out

    def exchange_start(e, value):
        face_out[e, 0] = value[:, : M // 2]
        face_out[e, 1] = value[:, M // 2 :]
        for side, target in ((0, left), (1, right)):
            copy = pltpu.make_async_remote_copy(
                src_ref=face_out.at[e, side], dst_ref=face_in.at[e, 1 - side],
                send_sem=face_send.at[e, side], recv_sem=face_recv.at[e, 1 - side],
                device_id=(target, g), device_id_type=MESH,
            )
            copy.start()
            started.append(copy)

    def exchange_end(e):
        for side, target in ((0, left), (1, right)):
            pltpu.make_async_remote_copy(
                src_ref=face_out.at[e, side], dst_ref=face_in.at[e, 1 - side],
                send_sem=face_send.at[e, side], recv_sem=face_recv.at[e, 1 - side],
                device_id=(target, g), device_id_type=MESH,
            ).wait_recv()
        first = face_out[e, 0] + face_in[e, 0]
        second = face_out[e, 1] + face_in[e, 1]
        return jnp.concatenate([first, second], 1)

    blocks = (
        lax.broadcasted_iota(jnp.int32, (8, M), 1) // BW
        == lax.broadcasted_iota(jnp.int32, (8, M), 0)
    ).astype(F32)
    sub = lax.broadcasted_iota(jnp.int32, (8, BW), 0)
    ones = jnp.ones((8, M), F32)
    pad = jnp.zeros((8, BW - R), F32)

    def averages(w):
        t = dot_hi(blocks, w, ((1,), (1,))) * (1.0 / ROOT)
        return jnp.concatenate([t, pad], 1)

    def sums_of(u, v):
        t = dot_hi(ones, u * v, ((1,), (1,)))
        return jnp.concatenate([t, pad], 1)

    def per_row(line):
        tile = jnp.where(sub == 0, jnp.broadcast_to(line, (8, BW)), 0.0)
        wide = dot_hi(tile, jnp.ones((8, BW), F32), ((0,), (0,)))[:R]
        return jnp.concatenate([wide] * NB, 1)

    def last_product(n):
        cols = slice(n * 256, (n + 1) * 256)
        xh_ref[:, cols], xl_ref[:, cols] = split(
            x_ref[:, cols] - dot(col_ref[...], rhs_ref[:, cols])
        )

    last_product(0)
    pl.semaphore_wait(barrier, len(partners))
    begin("avg", 2, tile_ref[...])
    exchange_start(4, loads_ref[...])
    for n in range(1, 4):
        last_product(n)
    right_side = exchange_end(4)
    weighted = 0.5 * right_side
    begin("avg", 0, averages(weighted))

    contributions = end("avg", 2)[2].reshape(n_grp * 8, BW)
    primal_all = contributions[:, C : 2 * C]
    local_all = contributions[:, :C]
    coarse = dot_hi(primal_all, local_all, ((0,), (0,)))
    coarse = coarse + (
        lax.broadcasted_iota(jnp.int32, (C, C), 0) == lax.broadcasted_iota(jnp.int32, (C, C), 1)
    ).astype(F32)
    coarse_inverse = dense_inverse(
        jnp.concatenate([coarse, jnp.zeros((C, BW - C), F32)], 1), C
    )[:, :C]
    primal = tile_ref[:, C : 2 * C]
    weights = dot_hi(dot_hi(primal, coarse_inverse, ((1,), (0,))), primal_all, ((1,), (1,)))

    def correction(e):
        gathered = end("avg", e)[e].reshape(n_grp * 8, BW)
        amounts = dot_hi(weights, gathered, ((1,), (0,))) * (1.0 / ROOT)
        return dot_hi(amounts[:, :R], blocks, ((0,), (0,)))

    solved = product(weighted, xh_ref, xl_ref)
    local_z = 0.5 * (solved + correction(0))
    exchange_start(0, local_z)
    rz = sums_of(right_side, local_z)
    z = exchange_end(0)

    prod = product(z, ah_ref, al_ref)
    exchange_start(1, prod)
    dp = sums_of(z, prod)
    begin("g", 0, jnp.where(sub == 0, rz, dp))
    image = exchange_end(1)

    half = 0.5 * image
    begin("avg", 1, averages(half))
    begin("x", 0, total("g", 0))
    solved_q = product(half, xh_ref, xl_ref)
    local_q = 0.5 * (solved_q + correction(1))
    exchange_start(2, local_q)
    begin("z", 0, total("x", 0))
    first = total("z", 0)
    rz0 = first[0:1]
    dp0 = first[1:2]
    alpha0 = rz0 / jnp.where(lax.broadcasted_iota(jnp.int32, (1, BW), 1) < R, dp0, 1.0)
    alpha0_rows = per_row(alpha0)
    residual = right_side - alpha0_rows * image
    rz = sums_of(residual, local_z - alpha0_rows * local_q)
    z1 = z - alpha0_rows * exchange_end(2)

    prod1 = product(z1, ah_ref, al_ref)
    exchange_start(3, prod1)
    zz = sums_of(z1, prod1)
    zd = sums_of(z1, prod)
    begin("g", 1, jnp.where(sub == 0, rz, jnp.where(sub == 1, zz, zd)))
    begin("x", 1, total("g", 1))
    image1 = exchange_end(3)
    begin("z", 1, total("x", 1))
    last = total("z", 1)
    valid = lax.broadcasted_iota(jnp.int32, (1, BW), 1) < R
    rz1 = last[0:1]
    beta = rz1 / jnp.where(valid, rz0, 1.0)
    energy = last[1:2] + 2.0 * beta * last[2:3] + beta * beta * dp0
    alpha1 = rz1 / jnp.where(valid, energy, 1.0)
    alpha1_rows = per_row(alpha1)
    beta_rows = per_row(beta)
    sol_ref[...] = alpha0_rows * z + alpha1_rows * (z1 + beta_rows * z)
    res_ref[...] = residual - alpha1_rows * (image1 + beta_rows * image)
    for copy in started:
        copy.wait_send()


def iterate(n_grp, n_sub, *args):
    n_z = n_sub // X_DIM
    out = jax.ShapeDtypeStruct((R, M), F32)
    dma = pltpu.SemaphoreType.DMA
    return pl.pallas_call(
        iterate_kernel,
        out_shape=(out, out),
        in_specs=[vmem()] * 7,
        out_specs=(vmem(), vmem()),
        scratch_shapes=[
            pltpu.VMEM((M, M), BF16),
            pltpu.VMEM((M, M), BF16),
            pltpu.VMEM((5, 2, R, M // 2), F32),
            pltpu.VMEM((5, 2, R, M // 2), F32),
            pltpu.VMEM((3, n_grp, 8, BW), F32),
            pltpu.VMEM((2, n_grp, 8, BW), F32),
            pltpu.VMEM((2, X_DIM, 8, BW), F32),
            pltpu.VMEM((2, n_z, 8, BW), F32),
            dma((5, 2)),
            dma((5, 2)),
            dma((3, n_grp)),
            dma((3, n_grp)),
            dma((2, n_grp)),
            dma((2, n_grp)),
            dma((2, X_DIM)),
            dma((2, X_DIM)),
            dma((2, n_z)),
            dma((2, n_z)),
        ],
        compiler_params=pltpu.CompilerParams(
            collective_id=0, has_side_effects=True, vmem_limit_bytes=40 * MIB
        ),
        cost_estimate=pl.CostEstimate(
            flops=2_000_000_000, bytes_accessed=10 * MIB, transcendentals=0
        ),
        name="iterate",
    )(*args)


def body(schur, loads, block_map, primal_map, disk_mask):
    n_sub = lax.axis_size("sub")
    n_grp = lax.axis_size("grp")
    block_map = block_map[0]
    matrix = schur[0, 0]
    mask = disk_mask[0]
    face, tile = prepare(block_map, primal_map[0], matrix, loads[0, 0], mask)
    a_high, a_low, x_part, col, rhs = invert(block_map, matrix, mask)
    sol, res = iterate(n_grp, n_sub, face, tile, a_high, a_low, x_part, col, rhs)
    return sol[None, None], res[None, None]


def solution(mesh):
    in_specs = (
        P("sub", "grp", None, None),
        P("sub", "grp", None, None),
        P("sub", "grp", None),
        P("sub", "grp", None),
        P("sub", "grp", None),
    )
    out_specs = (P("sub", "grp", None, None), P("sub", "grp", None, None))
    return jax.shard_map(body, mesh=mesh, in_specs=in_specs, out_specs=out_specs, check_vma=False)
```

```python
import jax
import jax.numpy as jnp
from jax import lax
from jax.experimental import pallas as pl
from jax.experimental.pallas import tpu as pltpu
from jax.sharding import PartitionSpec as P

F32 = jnp.float32
BF16 = jnp.bfloat16
HI = lax.Precision.HIGHEST
MESH = pl.DeviceIdType.MESH
M = 1024
R = 64
BW = 128
NB = 8
C = 32
X_DIM = 4
FIRST = NB - 2
ROOT = BW ** 0.5
MIB = 1 << 20


def vmem():
    return pl.BlockSpec(memory_space=pltpu.VMEM)


def smem():
    return pl.BlockSpec(memory_space=pltpu.SMEM)


def split(value):
    high = value.astype(BF16)
    low = (value - high.astype(F32)).astype(BF16)
    return high, low


def dot(a, b):
    return jnp.dot(a, b, preferred_element_type=F32)


def dot_hi(a, b, dims):
    return lax.dot_general(a, b, (dims, ((), ())), precision=HI, preferred_element_type=F32)


def spread(v):
    return jnp.broadcast_to(v, (8, BW))


def recip(a):
    r = pltpu.reciprocal(a, approx=True)
    return r * (2.0 - a * r)


def small_mm(a, b):
    out = []
    for i in range(len(a)):
        row = []
        for j in range(len(b[0])):
            t = a[i][0] * b[0][j]
            for l in range(1, len(b)):
                t = t + a[i][l] * b[l][j]
            row.append(t)
        out.append(row)
    return out


def small_inverse(d):
    n = len(d)
    if n == 2:
        a, b, e = d[0][0], d[0][1], d[1][1]
        r = recip(a * e - b * b)
        o = -(b * r)
        return [[e * r, o], [o, a * r]]
    h = n // 2
    a = small_inverse([row[:h] for row in d[:h]])
    b = [row[h:] for row in d[:h]]
    t = small_mm(a, b)
    s = [[None] * h for _ in range(h)]
    for i in range(h):
        for j in range(i, h):
            u = b[0][i] * t[0][j]
            for l in range(1, h):
                u = u + b[l][i] * t[l][j]
            s[i][j] = d[h + i][h + j] - u
            s[j][i] = s[i][j]
    s = small_inverse(s)
    ts = small_mm(t, s)
    r = [[None] * n for _ in range(n)]
    for i in range(h):
        for j in range(h):
            r[h + i][h + j] = s[i][j]
            r[i][h + j] = -ts[i][j]
            r[h + j][i] = r[i][h + j]
    for i in range(h):
        for j in range(i, h):
            u = a[i][j]
            for l in range(h):
                u = u + ts[i][l] * t[j][l]
            r[i][j] = u
            r[j][i] = u
    return r


def dense_inverse(x, n, beside=()):
    beside = list(beside)
    groups = n // 8
    xs = [x[8 * i : 8 * i + 8, :] for i in range(groups)]
    lane = lax.broadcasted_iota(jnp.int32, (8, BW), 1)
    sub = lax.broadcasted_iota(jnp.int32, (8, BW), 0)
    for q in range(groups):
        k = 8 * q
        rows = [spread(xs[q][j : j + 1, :]) for j in range(8)]
        d = [[None] * 8 for _ in range(8)]
        for i in range(8):
            for j in range(i, 8):
                d[i][j] = spread(rows[i][:, k + j : k + j + 1])
                d[j][i] = d[i][j]
        cols = [[spread(xs[i][:, k + j : k + j + 1]) for j in range(8)] for i in range(groups)]
        r = small_inverse(d)
        p = []
        for i in range(8):
            u = r[i][0] * rows[0]
            for j in range(1, 8):
                u = u + r[i][j] * rows[j]
            for j in range(8):
                u = jnp.where(lane == k + j, r[i][j], u)
            p.append(u)
        pivots = (lane >= k) & (lane < k + 8)
        new = []
        for i in range(groups):
            if i == q:
                y = p[0]
                for j in range(1, 8):
                    y = jnp.where(sub == j, p[j], y)
            else:
                y = jnp.where(pivots, 0.0, xs[i])
                for j in range(8):
                    y = y - cols[i][j] * p[j]
            new.append(y)
        xs = new
        if beside:
            beside.pop(0)()
    for work in beside:
        work()
    return jnp.concatenate(xs, 0)


def face_sources(bm_ref):
    places = [bm_ref[0, j] for j in range(NB)]
    out = []
    for f in range(NB):
        where = jnp.int32(0)
        for j in range(NB):
            where = where + jnp.where(places[j] == f, jnp.int32(j), jnp.int32(0))
        out.append(where)
    return out


def at(k):
    return pl.ds(pl.multiple_of(k * BW, BW), BW)


def four(value, axis):
    high, low = split(value)
    parts = [high, low, high, low] if axis == 1 else [high, high, low, low]
    return jnp.concatenate(parts, axis)


def elimination(x, col, rhs, panel, inv, here):
    def rows():
        panel[...] = dot(four(inv[...], 1), four(x[here, :M], 0))
        col[...] = four(x[:M, here], 1)
        x[:, here] = jnp.zeros((x.shape[0], BW), F32)
        rhs[:, :M] = four(panel[...], 0)
        rhs[:, here] = four(inv[...], 0)

    def block(n):
        cols = slice(n * 256, (n + 1) * 256)

        def work():
            x[:M, cols] = x[:M, cols] - dot(col[...], rhs[:, cols])

        return work

    def finish():
        x[here, :M] = panel[...]
        x[here, here] = inv[...]

    return rows, [block(n) for n in range(4)], finish


def nothing():
    pass


def pivot_step(x, col, rhs, panel, inv, pivot, last, here, after):
    rows, blocks, finish = elimination(x, col, rhs, panel, inv, last)
    rows()
    work = []
    for block in blocks:
        work += [block, nothing, nothing]
    inverse = dense_inverse(pivot[...], BW, work)
    finish()
    inv[...] = inverse
    if after is not None:
        p = dot(four(inverse, 1), four(x[here, after], 0))
        pivot[...] = x[after, after] - dot(four(x[after, here], 1), four(p, 0))


def invert_kernel(
    bm_ref, pm_ref, schur_ref, loads_ref, mask_ref,
    ah_ref, al_ref, x, inv, pivot, face_ref, tile_ref,
    col, rhs, panel, sums,
):
    source = face_sources(bm_ref)
    eye = lax.broadcasted_iota(jnp.int32, (BW, BW), 0) == lax.broadcasted_iota(
        jnp.int32, (BW, BW), 1
    )
    for f in range(NB):
        row_at = pl.multiple_of(source[f] * BW, BW)
        face_ref[:, f * BW : (f + 1) * BW] = loads_ref[:, pl.ds(row_at, BW)]
        for h in range(NB):
            col_at = pl.multiple_of(source[h] * BW, BW)
            block = schur_ref[pl.ds(row_at, BW), pl.ds(col_at, BW)]
            if f == h:
                penalty = 0.1 * mask_ref[:, pl.ds(col_at, BW)].astype(F32)
                block = block + jnp.where(eye, penalty, 0.0)
            x[f * BW : (f + 1) * BW, h * BW : (h + 1) * BW] = block
            sums[f : f + 1, h * BW : (h + 1) * BW] = jnp.sum(block, axis=0, keepdims=True)
            high, low = split(block)
            ah_ref[f * BW : (f + 1) * BW, h * BW : (h + 1) * BW] = high
            al_ref[f * BW : (f + 1) * BW, h * BW : (h + 1) * BW] = low
    x[M:, :] = jnp.zeros((BW, M + BW), F32)
    x[:M, M:] = jnp.zeros((M, BW), F32)
    inv[...] = jnp.zeros((BW, BW), F32)
    pivot[...] = x[0:BW, 0:BW]

    sub = lax.broadcasted_iota(jnp.int32, (8, BW), 0)
    lane = lax.broadcasted_iota(jnp.int32, (8, BW), 1)
    primal = jnp.zeros((8, BW), F32)
    shifted = jnp.zeros((8, BW), F32)
    for f in range(NB):
        coarse = pm_ref[0, source[f]]
        primal = jnp.where((sub == f) & (lane == coarse), 1.0, primal)
        shifted = jnp.where((sub == f) & (lane == coarse + C), 1.0, shifted)
    block_sums = dot_hi(sums[...], block_indicator(), ((1,), (1,))) / BW
    tile_ref[...] = dot_hi(block_sums, primal, ((1,), (0,))) + shifted

    def step(k, carry):
        last = at(lax.rem(k + NB, NB + 1))
        pivot_step(x, col, rhs, panel, inv, pivot, last, at(k), at(k + 1))
        return carry

    lax.fori_loop(0, FIRST, step, 0)


def invert(block_map, primal_map, schur, loads, mask):
    def arr(shape, dtype=F32):
        return jax.ShapeDtypeStruct(shape, dtype)

    return pl.pallas_call(
        invert_kernel,
        out_shape=(
            arr((M, M), BF16), arr((M, M), BF16), arr((M + BW, M + BW)), arr((BW, BW)),
            arr((BW, BW)), arr((R, M)), arr((8, BW)),
        ),
        in_specs=[smem(), smem(), vmem(), vmem(), vmem()],
        out_specs=(vmem(),) * 7,
        scratch_shapes=[
            pltpu.VMEM((M, 4 * BW), BF16),
            pltpu.VMEM((4 * BW, M + BW), BF16),
            pltpu.VMEM((BW, M), F32),
            pltpu.VMEM((8, M), F32),
        ],
        compiler_params=pltpu.CompilerParams(vmem_limit_bytes=40 * MIB),
        cost_estimate=pl.CostEstimate(
            flops=20_000_000_000, bytes_accessed=12 * MIB, transcendentals=0
        ),
        name="invert",
    )(block_map, primal_map, schur, loads, mask)


def block_indicator():
    return (
        lax.broadcasted_iota(jnp.int32, (8, M), 1) // BW
        == lax.broadcasted_iota(jnp.int32, (8, M), 0)
    ).astype(F32)


def product(value, high_ref, low_ref):
    high, low = split(value)
    both = dot(jnp.concatenate([high, low], 0), high_ref[...])
    return both[:R] + both[R:] + dot(high, low_ref[...])


def iterate_kernel(
    loads_ref, tile_ref, ah_ref, al_ref, x_ref, inv_ref, pivot_ref,
    sol_ref, res_ref,
    xh_ref, xl_ref, x, col, rhs, panel, inv, pivot,
    face_out, face_in, tiles, avg, weights_out, weights_in, sum_gx, sum_z,
    face_send, face_recv, tile_send, tile_recv, avg_send, avg_recv, w_send, w_recv,
    gx_send, gx_recv, z_send, z_recv,
):
    s = lax.axis_index("sub")
    g = lax.axis_index("grp")
    n_sub = lax.axis_size("sub")
    n_grp = lax.axis_size("grp")
    n_z = n_sub // X_DIM
    n_gx = n_grp * X_DIM
    xi = lax.rem(s, X_DIM)
    zi = s // X_DIM
    left = lax.rem(s + n_sub - 1, n_sub)
    right = lax.rem(s + 1, n_sub)
    mine = xi * n_grp + g

    def around(d):
        return lax.rem(g + d, n_grp)

    def gx_peer(d):
        return (zi * X_DIM + lax.rem(xi + d // n_grp, X_DIM), around(d % n_grp))

    def gx_slot(d):
        return lax.rem(xi + d // n_grp, X_DIM) * n_grp + around(d % n_grp)

    def z_peer(d):
        return (lax.rem(zi + d, n_z) * X_DIM + xi, g)

    partners = [(left, around(d)) for d in range(n_grp)]
    partners += [(right, around(d)) for d in range(n_grp)]
    partners += [gx_peer(d) for d in range(1, n_gx)]
    partners += [z_peer(d) for d in range(1, n_z)]
    barrier = pltpu.get_barrier_semaphore()
    for partner in partners:
        pl.semaphore_signal(barrier, inc=1, device_id=partner, device_id_type=MESH)

    started = []

    def copy_of(src, dst, send, recv, target):
        return pltpu.make_async_remote_copy(
            src_ref=src, dst_ref=dst, send_sem=send, recv_sem=recv,
            device_id=target, device_id_type=MESH,
        )

    def start(*args):
        copy = copy_of(*args)
        copy.start()
        started.append(copy)

    def wait(*args):
        copy_of(*args).wait_recv()

    def gx_begin(e, tile):
        sum_gx[e, mine] = tile
        for d in range(1, n_gx):
            start(
                sum_gx.at[e, mine], sum_gx.at[e, mine],
                gx_send.at[e, d], gx_recv.at[e, mine], gx_peer(d),
            )

    def gx_total(e):
        for d in range(1, n_gx):
            o = gx_slot(d)
            wait(sum_gx.at[e, o], sum_gx.at[e, o], gx_send.at[e, d], gx_recv.at[e, o], gx_peer(d))
        return jnp.sum(sum_gx[e], axis=0)

    def z_begin(e, tile):
        sum_z[e, zi] = tile
        for d in range(1, n_z):
            start(
                sum_z.at[e, zi], sum_z.at[e, zi], z_send.at[e, d], z_recv.at[e, zi], z_peer(d)
            )

    def z_total(e):
        for d in range(1, n_z):
            o = lax.rem(zi + d, n_z)
            wait(sum_z.at[e, o], sum_z.at[e, o], z_send.at[e, d], z_recv.at[e, o], z_peer(d))
        return jnp.sum(sum_z[e], axis=0)

    def avg_begin(e, tile):
        avg[e, 0, g] = tile
        for d in range(1, n_grp):
            start(
                avg.at[e, 0, g], avg.at[e, 0, g],
                avg_send.at[e, 0, d], avg_recv.at[e, 0, g], (s, around(d)),
            )
        for side, target in ((1, right), (2, left)):
            for d in range(n_grp):
                start(
                    avg.at[e, 0, g], avg.at[e, side, g],
                    avg_send.at[e, side, d], avg_recv.at[e, side, g], (target, around(d)),
                )

    def avg_end(e):
        for side, target in ((0, s), (1, right), (2, left)):
            for d in range(0 if side else 1, n_grp):
                o = around(d)
                wait(
                    avg.at[e, side, o], avg.at[e, side, o],
                    avg_send.at[e, side, d], avg_recv.at[e, side, o], (target, o),
                )

    def face_args(e, side):
        return (
            face_out.at[e, side], face_in.at[e, 1 - side],
            face_send.at[e, side], face_recv.at[e, 1 - side],
            ((left, right)[side], g),
        )

    def exchange_start(e, value):
        face_out[e, 0] = value[:, : M // 2]
        face_out[e, 1] = value[:, M // 2 :]
        for side in range(2):
            start(*face_args(e, side))

    def exchange_end(e):
        for side in range(2):
            wait(*face_args(e, side))
        first = face_out[e, 0] + face_in[e, 0]
        second = face_out[e, 1] + face_in[e, 1]
        return jnp.concatenate([first, second], 1)

    blocks = block_indicator()
    sub = lax.broadcasted_iota(jnp.int32, (8, BW), 0)
    ones = jnp.ones((8, M), F32)
    pad = jnp.zeros((8, BW - R), F32)

    def averages(w):
        t = dot_hi(blocks, w, ((1,), (1,))) * (1.0 / ROOT)
        return jnp.concatenate([t, pad], 1)

    def sums_of(u, v):
        t = dot_hi(ones, u * v, ((1,), (1,)))
        return jnp.concatenate([t, pad], 1)

    def per_row(line):
        tile = jnp.where(sub == 0, jnp.broadcast_to(line, (8, BW)), 0.0)
        wide = dot_hi(tile, jnp.ones((8, BW), F32), ((0,), (0,)))[:R]
        return jnp.concatenate([wide] * NB, 1)

    def piece(k):
        return slice(k * BW, (k + 1) * BW)

    x[...] = x_ref[:M, :M]
    inv[...] = inv_ref[...]
    pivot[...] = pivot_ref[...]
    pivot_step(
        x, col, rhs, panel, inv, pivot, piece(NB - 3), piece(NB - 2), piece(NB - 1)
    )
    pl.semaphore_wait(barrier, len(partners))
    tiles[g] = tile_ref[...]
    for d in range(1, n_grp):
        start(tiles.at[g], tiles.at[g], tile_send.at[d], tile_recv.at[g], (s, around(d)))
    exchange_start(4, loads_ref[...])
    pivot_step(x, col, rhs, panel, inv, pivot, piece(NB - 2), piece(NB - 1), None)
    rows, _, finish = elimination(x, col, rhs, panel, inv, piece(NB - 1))
    rows()
    finish()
    col[M - BW :, :] = jnp.zeros((BW, 4 * BW), BF16)

    for d in range(1, n_grp):
        o = around(d)
        wait(tiles.at[o], tiles.at[o], tile_send.at[d], tile_recv.at[o], (s, o))
    contributions = tiles[...].reshape(n_grp * 8, BW)
    primal_all = contributions[:, C : 2 * C]
    local_all = contributions[:, :C]
    coarse = dot_hi(primal_all, local_all, ((0,), (0,)))
    coarse = coarse + (
        lax.broadcasted_iota(jnp.int32, (C, C), 0) == lax.broadcasted_iota(jnp.int32, (C, C), 1)
    ).astype(F32)
    coarse_inverse = dense_inverse(
        jnp.concatenate([coarse, jnp.zeros((C, BW - C), F32)], 1), C
    )[:, :C]
    primal = tile_ref[:, C : 2 * C]
    weights = dot_hi(dot_hi(primal, coarse_inverse, ((1,), (0,))), primal_all, ((1,), (1,)))
    for n in range(4):
        cols = slice(n * 256, (n + 1) * 256)
        xh_ref[:, cols], xl_ref[:, cols] = split(x[:, cols] - dot(col[...], rhs[:, cols]))

    def weight_args(side):
        return (
            weights_out, weights_in.at[1 - side], w_send.at[side], w_recv.at[1 - side],
            ((left, right)[side], g),
        )

    weights_out[...] = jnp.concatenate([weights, jnp.zeros((8, BW - n_grp * 8), F32)], 1)
    for side in range(2):
        start(*weight_args(side))

    def amounts(e):
        avg_end(e)
        part = [
            dot_hi(w, avg[e, side].reshape(n_grp * 8, BW), ((1,), (0,))) * (1.0 / ROOT)
            for side, w in enumerate(weight_sides)
        ]
        return part[0], part[0] + part[1] + part[2]

    def expand(tile):
        return dot_hi(tile[:, :R], blocks, ((0,), (0,)))

    right_side = exchange_end(4)
    weighted = 0.5 * right_side
    mean = averages(weighted)
    avg_begin(0, mean)

    local_z = 0.5 * product(weighted, xh_ref, xl_ref)
    exchange_start(0, local_z)
    for side in range(2):
        wait(*weight_args(side))
    swapped = [pltpu.roll(weights_in[side], 4, 0)[:, : n_grp * 8] for side in range(2)]
    upper = lax.broadcasted_iota(jnp.int32, (8, n_grp * 8), 0) < 4
    weight_sides = [
        weights,
        jnp.where(upper, swapped[0], 0.0),
        jnp.where(upper, 0.0, swapped[1]),
    ]
    own, both = amounts(0)
    rz = sums_of(right_side, local_z) + ROOT * jnp.sum(own * mean, axis=0, keepdims=True)
    coarse_z = 0.5 * expand(both)
    z = exchange_end(0) + coarse_z

    prod = product(z, ah_ref, al_ref)
    exchange_start(1, prod)
    dp = sums_of(z, prod)
    gx_begin(0, jnp.where(sub == 0, rz, dp))
    image = exchange_end(1)

    half = 0.5 * image
    mean_q = averages(half)
    avg_begin(1, mean_q)
    local_q = 0.5 * product(half, xh_ref, xl_ref)
    exchange_start(2, local_q)
    z_begin(0, gx_total(0))
    own_q, both_q = amounts(1)
    coarse_q = 0.5 * expand(both_q)
    q = exchange_end(2) + coarse_q
    first = z_total(0)
    valid = lax.broadcasted_iota(jnp.int32, (1, BW), 1) < R
    rz0 = first[0:1]
    dp0 = first[1:2]
    alpha0 = rz0 / jnp.where(valid, dp0, 1.0)
    alpha0_rows = per_row(alpha0)
    z1 = z - alpha0_rows * q

    prod1 = product(z1, ah_ref, al_ref)
    exchange_start(3, prod1)
    residual = right_side - alpha0_rows * image
    rz = sums_of(residual, local_z - alpha0_rows * local_q) + ROOT * jnp.sum(
        (own - alpha0 * own_q) * (mean - alpha0 * mean_q), axis=0, keepdims=True
    )
    zz = sums_of(z1, prod1)
    zd = sums_of(z1, prod)
    gx_begin(1, jnp.where(sub == 0, rz, jnp.where(sub == 1, zz, zd)))
    z_begin(1, gx_total(1))
    image1 = exchange_end(3)
    last = z_total(1)
    rz1 = last[0:1]
    beta = rz1 / jnp.where(valid, rz0, 1.0)
    energy = last[1:2] + 2.0 * beta * last[2:3] + beta * beta * dp0
    alpha1 = rz1 / jnp.where(valid, energy, 1.0)
    alpha1_rows = per_row(alpha1)
    beta_rows = per_row(beta)
    sol_ref[...] = alpha0_rows * z + alpha1_rows * (z1 + beta_rows * z)
    res_ref[...] = residual - alpha1_rows * (image1 + beta_rows * image)
    for copy in started:
        copy.wait_send()


def iterate(n_grp, n_sub, *args):
    n_z = n_sub // X_DIM
    n_gx = n_grp * X_DIM
    out = jax.ShapeDtypeStruct((R, M), F32)
    dma = pltpu.SemaphoreType.DMA
    return pl.pallas_call(
        iterate_kernel,
        out_shape=(out, out),
        in_specs=[vmem()] * len(args),
        out_specs=(vmem(), vmem()),
        scratch_shapes=[
            pltpu.VMEM((M, M), BF16),
            pltpu.VMEM((M, M), BF16),
            pltpu.VMEM((M, M), F32),
            pltpu.VMEM((M, 4 * BW), BF16),
            pltpu.VMEM((4 * BW, M), BF16),
            pltpu.VMEM((BW, M), F32),
            pltpu.VMEM((BW, BW), F32),
            pltpu.VMEM((BW, BW), F32),
            pltpu.VMEM((5, 2, R, M // 2), F32),
            pltpu.VMEM((5, 2, R, M // 2), F32),
            pltpu.VMEM((n_grp, 8, BW), F32),
            pltpu.VMEM((2, 3, n_grp, 8, BW), F32),
            pltpu.VMEM((8, BW), F32),
            pltpu.VMEM((2, 8, BW), F32),
            pltpu.VMEM((2, n_gx, 8, BW), F32),
            pltpu.VMEM((2, n_z, 8, BW), F32),
            dma((5, 2)),
            dma((5, 2)),
            dma((n_grp,)),
            dma((n_grp,)),
            dma((2, 3, n_grp)),
            dma((2, 3, n_grp)),
            dma((2,)),
            dma((2,)),
            dma((2, n_gx)),
            dma((2, n_gx)),
            dma((2, n_z)),
            dma((2, n_z)),
        ],
        compiler_params=pltpu.CompilerParams(
            collective_id=0, has_side_effects=True, vmem_limit_bytes=40 * MIB
        ),
        cost_estimate=pl.CostEstimate(
            flops=2_000_000_000, bytes_accessed=10 * MIB, transcendentals=0
        ),
        name="iterate",
    )(*args)


def body(schur, loads, block_map, primal_map, disk_mask):
    a_high, a_low, x, inv, pivot, face, tile = invert(
        block_map[0], primal_map[0], schur[0, 0], loads[0, 0], disk_mask[0]
    )
    sol, res = iterate(
        lax.axis_size("grp"), lax.axis_size("sub"), face, tile, a_high, a_low, x, inv, pivot
    )
    return sol[None, None], res[None, None]


def solution(mesh):
    in_specs = (
        P("sub", "grp", None, None),
        P("sub", "grp", None, None),
        P("sub", "grp", None),
        P("sub", "grp", None),
        P("sub", "grp", None),
    )
    out_specs = (P("sub", "grp", None, None), P("sub", "grp", None, None))
    return jax.shard_map(body, mesh=mesh, in_specs=in_specs, out_specs=out_specs, check_vma=False)
```

```python
import jax
import jax.numpy as jnp
from jax import lax
from jax.experimental import pallas as pl
from jax.experimental.pallas import tpu as pltpu
from jax.sharding import PartitionSpec as P

F32 = jnp.float32
BF16 = jnp.bfloat16
HI = lax.Precision.HIGHEST
MESH = pl.DeviceIdType.MESH
M = 1024
R = 64
BW = 128
NB = 8
C = 32
X_DIM = 4
FIRST = NB - 2
ROOT = BW ** 0.5
LOWEST = -3e38
MIB = 1 << 20


def vmem():
    return pl.BlockSpec(memory_space=pltpu.VMEM)


def smem():
    return pl.BlockSpec(memory_space=pltpu.SMEM)


def split(value):
    high = value.astype(BF16)
    low = (value - high.astype(F32)).astype(BF16)
    return high, low


def dot(a, b):
    return jnp.dot(a, b, preferred_element_type=F32)


def dot_hi(a, b, dims):
    return lax.dot_general(a, b, (dims, ((), ())), precision=HI, preferred_element_type=F32)


def spread(v):
    return jnp.broadcast_to(v, (8, BW))


def column_inverse(c, sub):
    for j in range(0, 8, 2):
        at_a, at_b = sub == j, sub == j + 1
        fa, fb = c[j], c[j + 1]
        a = spread(fa[j : j + 1, :])
        b = spread(fb[j : j + 1, :])
        e = spread(fb[j + 1 : j + 2, :])
        det = a * e - b * b
        r1 = pltpu.reciprocal(det, approx=True)
        t = 2.0 - det * r1
        r = r1 * t
        new = []
        for l in range(8):
            if l == j:
                v = fa * e - fb * b
                new.append(jnp.where(at_a, e * r, jnp.where(at_b, -(b * r), -(v * r))))
            elif l == j + 1:
                v = fb * a - fa * b
                new.append(jnp.where(at_a, -(b * r), jnp.where(at_b, a * r, -(v * r))))
            else:
                ra = spread(c[l][j : j + 1, :])
                rb = spread(c[l][j + 1 : j + 2, :])
                ua = e * ra - b * rb
                ub = a * rb - b * ra
                v = fa * ua + fb * ub
                rest = c[l] - (v * r1) * t
                new.append(jnp.where(at_a, ua * r, jnp.where(at_b, ub * r, rest)))
        c = new
    return c


def dense_inverse(x, n, beside=()):
    beside = list(beside)
    groups = n // 8
    xs = [x[8 * i : 8 * i + 8, :] for i in range(groups)]
    lane = lax.broadcasted_iota(jnp.int32, (8, BW), 1)
    sub = lax.broadcasted_iota(jnp.int32, (8, BW), 0)
    for q in range(groups):
        k = 8 * q
        others = [(q + 1 + i) % groups for i in range(groups - 1)]
        own = [jnp.maximum(spread(xs[q][:, k + j : k + j + 1]), LOWEST) for j in range(8)]
        cols = {i: [spread(xs[i][:, k + j : k + j + 1]) for j in range(8)] for i in others}
        pivots = (lane >= k) & (lane < k + 8)
        r = column_inverse(own, sub)
        rows = [
            jnp.where(pivots, (lane == k + j).astype(F32), spread(xs[q][j : j + 1, :]))
            for j in range(8)
        ]
        p = r[0] * rows[0]
        for j in range(1, 8):
            p = p + r[j] * rows[j]
        lines = [spread(p[j : j + 1, :]) for j in range(8)]
        new = [None] * groups
        new[q] = p
        for i in others:
            y = jnp.where(pivots, 0.0, xs[i])
            for j in range(8):
                y = y - cols[i][j] * lines[j]
            new[i] = y
        xs = new
        if beside:
            beside.pop(0)()
    for work in beside:
        work()
    return jnp.concatenate(xs, 0)


def face_sources(bm_ref):
    places = [bm_ref[0, j] for j in range(NB)]
    out = []
    for f in range(NB):
        where = jnp.int32(0)
        for j in range(NB):
            where = where + jnp.where(places[j] == f, jnp.int32(j), jnp.int32(0))
        out.append(where)
    return out


def at(k):
    return pl.ds(pl.multiple_of(k * BW, BW), BW)


def four(value, axis):
    high, low = split(value)
    parts = [high, low, high, low] if axis == 1 else [high, high, low, low]
    return jnp.concatenate(parts, axis)


def elimination(x, col, rhs, panel, inv, here):
    def rows():
        panel[...] = dot(four(inv[...], 1), four(x[here, :], 0))
        col[...] = four(x[:, here], 1)
        x[:, here] = jnp.zeros((x.shape[0], BW), F32)
        rhs[...] = four(panel[...], 0)
        rhs[:, here] = four(inv[...], 0)

    def block(n):
        cols = slice(n * 256, (n + 1) * 256)

        def work():
            x[:, cols] = x[:, cols] - dot(col[...], rhs[:, cols])

        return work

    def finish():
        x[here, :] = panel[...]
        x[here, here] = inv[...]

    return rows, [block(n) for n in range(4)], finish


def nothing():
    pass


def next_pivot(x, inv, pivot, inverse, here, after):
    inv[...] = inverse
    p = dot(four(inverse, 1), four(x[here, after], 0))
    pivot[...] = x[after, after] - dot(four(x[after, here], 1), four(p, 0))


def pivot_step(x, col, rhs, panel, inv, pivot, last, here, after):
    rows, blocks, finish = elimination(x, col, rhs, panel, inv, last)
    rows()
    work = []
    for block in blocks:
        work += [block, nothing, nothing]
    inverse = dense_inverse(pivot[...], BW, work)
    finish()
    if after is None:
        inv[...] = inverse
    else:
        next_pivot(x, inv, pivot, inverse, here, after)


def invert_kernel(
    bm_ref, pm_ref, schur_ref, loads_ref, mask_ref,
    ah_ref, al_ref, x, inv, pivot, face_ref, tile_ref,
    col, rhs, panel, sums,
):
    source = face_sources(bm_ref)
    eye = lax.broadcasted_iota(jnp.int32, (BW, BW), 0) == lax.broadcasted_iota(
        jnp.int32, (BW, BW), 1
    )

    def load(f, h):
        row_at = pl.multiple_of(source[f] * BW, BW)
        col_at = pl.multiple_of(source[h] * BW, BW)
        block = schur_ref[pl.ds(row_at, BW), pl.ds(col_at, BW)]
        if f == h:
            penalty = 0.1 * mask_ref[:, pl.ds(col_at, BW)].astype(F32)
            block = block + jnp.where(eye, penalty, 0.0)
        return block

    def place(f):
        def work():
            rows = slice(f * BW, (f + 1) * BW)
            at_f = pl.multiple_of(source[f] * BW, BW)
            face_ref[:, rows] = loads_ref[:, pl.ds(at_f, BW)]
            for h in range(NB):
                cols = slice(h * BW, (h + 1) * BW)
                block = load(f, h)
                x[rows, cols] = block
                sums[f : f + 1, cols] = jnp.sum(block, axis=0, keepdims=True)
                ah_ref[rows, cols], al_ref[rows, cols] = split(block)

        return work

    first = slice(0, BW)
    inverse = dense_inverse(load(0, 0), BW, [place(f) for f in range(NB)])
    next_pivot(x, inv, pivot, inverse, first, slice(BW, 2 * BW))

    sub = lax.broadcasted_iota(jnp.int32, (8, BW), 0)
    lane = lax.broadcasted_iota(jnp.int32, (8, BW), 1)
    primal = jnp.zeros((8, BW), F32)
    shifted = jnp.zeros((8, BW), F32)
    for f in range(NB):
        coarse = pm_ref[0, source[f]]
        primal = jnp.where((sub == f) & (lane == coarse), 1.0, primal)
        shifted = jnp.where((sub == f) & (lane == coarse + C), 1.0, shifted)
    block_sums = dot_hi(sums[...], block_indicator(), ((1,), (1,))) / BW
    tile_ref[...] = dot_hi(block_sums, primal, ((1,), (0,))) + shifted

    def step(k, carry):
        pivot_step(x, col, rhs, panel, inv, pivot, at(k - 1), at(k), at(k + 1))
        return carry

    lax.fori_loop(1, FIRST, step, 0)


def invert(block_map, primal_map, schur, loads, mask):
    def arr(shape, dtype=F32):
        return jax.ShapeDtypeStruct(shape, dtype)

    return pl.pallas_call(
        invert_kernel,
        out_shape=(
            arr((M, M), BF16), arr((M, M), BF16), arr((M, M)), arr((BW, BW)),
            arr((BW, BW)), arr((R, M)), arr((8, BW)),
        ),
        in_specs=[smem(), smem(), vmem(), vmem(), vmem()],
        out_specs=(vmem(),) * 7,
        scratch_shapes=[
            pltpu.VMEM((M, 4 * BW), BF16),
            pltpu.VMEM((4 * BW, M), BF16),
            pltpu.VMEM((BW, M), F32),
            pltpu.VMEM((8, M), F32),
        ],
        compiler_params=pltpu.CompilerParams(vmem_limit_bytes=40 * MIB),
        cost_estimate=pl.CostEstimate(
            flops=20_000_000_000, bytes_accessed=12 * MIB, transcendentals=0
        ),
        name="invert",
    )(block_map, primal_map, schur, loads, mask)


def block_indicator():
    return (
        lax.broadcasted_iota(jnp.int32, (8, M), 1) // BW
        == lax.broadcasted_iota(jnp.int32, (8, M), 0)
    ).astype(F32)


def product(value, high_ref, low_ref):
    high, low = split(value)
    both = dot(jnp.concatenate([high, low], 0), high_ref[...])
    return both[:R] + both[R:] + dot(high, low_ref[...])


def iterate_kernel(
    loads_ref, tile_ref, ah_ref, al_ref, x_ref, inv_ref, pivot_ref,
    sol_ref, res_ref,
    xh_ref, xl_ref, x, col, rhs, panel, inv, pivot,
    face_out, face_in, tiles, avg, weights_out, weights_in, sum_gx, sum_z,
    face_send, face_recv, tile_send, tile_recv, avg_send, avg_recv, w_send, w_recv,
    gx_send, gx_recv, z_send, z_recv,
):
    s = lax.axis_index("sub")
    g = lax.axis_index("grp")
    n_sub = lax.axis_size("sub")
    n_grp = lax.axis_size("grp")
    n_z = n_sub // X_DIM
    n_gx = n_grp * X_DIM
    xi = lax.rem(s, X_DIM)
    zi = s // X_DIM
    left = lax.rem(s + n_sub - 1, n_sub)
    right = lax.rem(s + 1, n_sub)
    mine = xi * n_grp + g

    def around(d):
        return lax.rem(g + d, n_grp)

    def gx_peer(d):
        return (zi * X_DIM + lax.rem(xi + d // n_grp, X_DIM), around(d % n_grp))

    def gx_slot(d):
        return lax.rem(xi + d // n_grp, X_DIM) * n_grp + around(d % n_grp)

    def z_peer(d):
        return (lax.rem(zi + d, n_z) * X_DIM + xi, g)

    partners = [(left, around(d)) for d in range(n_grp)]
    partners += [(right, around(d)) for d in range(n_grp)]
    partners += [gx_peer(d) for d in range(1, n_gx)]
    partners += [z_peer(d) for d in range(1, n_z)]
    barrier = pltpu.get_barrier_semaphore()
    for partner in partners:
        pl.semaphore_signal(barrier, inc=1, device_id=partner, device_id_type=MESH)

    started = []

    def copy_of(src, dst, send, recv, target):
        return pltpu.make_async_remote_copy(
            src_ref=src, dst_ref=dst, send_sem=send, recv_sem=recv,
            device_id=target, device_id_type=MESH,
        )

    def start(*args):
        copy = copy_of(*args)
        copy.start()
        started.append(copy)

    def wait(*args):
        copy_of(*args).wait_recv()

    def gx_begin(e, tile):
        sum_gx[e, mine] = tile
        for d in range(1, n_gx):
            start(
                sum_gx.at[e, mine], sum_gx.at[e, mine],
                gx_send.at[e, d], gx_recv.at[e, mine], gx_peer(d),
            )

    def gx_total(e):
        for d in range(1, n_gx):
            o = gx_slot(d)
            wait(sum_gx.at[e, o], sum_gx.at[e, o], gx_send.at[e, d], gx_recv.at[e, o], gx_peer(d))
        return jnp.sum(sum_gx[e], axis=0)

    def z_begin(e, tile):
        sum_z[e, zi] = tile
        for d in range(1, n_z):
            start(
                sum_z.at[e, zi], sum_z.at[e, zi], z_send.at[e, d], z_recv.at[e, zi], z_peer(d)
            )

    def z_total(e):
        for d in range(1, n_z):
            o = lax.rem(zi + d, n_z)
            wait(sum_z.at[e, o], sum_z.at[e, o], z_send.at[e, d], z_recv.at[e, o], z_peer(d))
        return jnp.sum(sum_z[e], axis=0)

    def avg_begin(e, tile):
        avg[e, 0, g] = tile
        for d in range(1, n_grp):
            start(
                avg.at[e, 0, g], avg.at[e, 0, g],
                avg_send.at[e, 0, d], avg_recv.at[e, 0, g], (s, around(d)),
            )
        for side, target in ((1, right), (2, left)):
            for d in range(n_grp):
                start(
                    avg.at[e, 0, g], avg.at[e, side, g],
                    avg_send.at[e, side, d], avg_recv.at[e, side, g], (target, around(d)),
                )

    def avg_end(e):
        for side, target in ((0, s), (1, right), (2, left)):
            for d in range(0 if side else 1, n_grp):
                o = around(d)
                wait(
                    avg.at[e, side, o], avg.at[e, side, o],
                    avg_send.at[e, side, d], avg_recv.at[e, side, o], (target, o),
                )

    def face_args(e, side):
        return (
            face_out.at[e, side], face_in.at[e, 1 - side],
            face_send.at[e, side], face_recv.at[e, 1 - side],
            ((left, right)[side], g),
        )

    def exchange_start(e, value):
        face_out[e, 0] = value[:, : M // 2]
        face_out[e, 1] = value[:, M // 2 :]
        for side in range(2):
            start(*face_args(e, side))

    def exchange_end(e):
        for side in range(2):
            wait(*face_args(e, side))
        first = face_out[e, 0] + face_in[e, 0]
        second = face_out[e, 1] + face_in[e, 1]
        return jnp.concatenate([first, second], 1)

    blocks = block_indicator()
    sub = lax.broadcasted_iota(jnp.int32, (8, BW), 0)
    ones = jnp.ones((8, M), F32)
    pad = jnp.zeros((8, BW - R), F32)

    def averages(w):
        t = dot_hi(blocks, w, ((1,), (1,))) * (1.0 / ROOT)
        return jnp.concatenate([t, pad], 1)

    def sums_of(u, v):
        t = dot_hi(ones, u * v, ((1,), (1,)))
        return jnp.concatenate([t, pad], 1)

    def per_row(line):
        tile = jnp.where(sub == 0, jnp.broadcast_to(line, (8, BW)), 0.0)
        wide = dot_hi(tile, jnp.ones((8, BW), F32), ((0,), (0,)))[:R]
        return jnp.concatenate([wide] * NB, 1)

    def piece(k):
        return slice(k * BW, (k + 1) * BW)

    x[...] = x_ref[...]
    inv[...] = inv_ref[...]
    pivot[...] = pivot_ref[...]
    pivot_step(
        x, col, rhs, panel, inv, pivot, piece(NB - 3), piece(NB - 2), piece(NB - 1)
    )
    pl.semaphore_wait(barrier, len(partners))
    tiles[g] = tile_ref[...]
    for d in range(1, n_grp):
        start(tiles.at[g], tiles.at[g], tile_send.at[d], tile_recv.at[g], (s, around(d)))
    exchange_start(4, loads_ref[...])
    pivot_step(x, col, rhs, panel, inv, pivot, piece(NB - 2), piece(NB - 1), None)
    rows, _, finish = elimination(x, col, rhs, panel, inv, piece(NB - 1))
    rows()
    finish()
    col[M - BW :, :] = jnp.zeros((BW, 4 * BW), BF16)

    for d in range(1, n_grp):
        o = around(d)
        wait(tiles.at[o], tiles.at[o], tile_send.at[d], tile_recv.at[o], (s, o))
    contributions = tiles[...].reshape(n_grp * 8, BW)
    primal_all = contributions[:, C : 2 * C]
    local_all = contributions[:, :C]
    coarse = dot_hi(primal_all, local_all, ((0,), (0,)))
    coarse = coarse + (
        lax.broadcasted_iota(jnp.int32, (C, C), 0) == lax.broadcasted_iota(jnp.int32, (C, C), 1)
    ).astype(F32)
    coarse_inverse = dense_inverse(
        jnp.concatenate([coarse, jnp.zeros((C, BW - C), F32)], 1), C
    )[:, :C]
    primal = tile_ref[:, C : 2 * C]
    weights = dot_hi(dot_hi(primal, coarse_inverse, ((1,), (0,))), primal_all, ((1,), (1,)))
    for n in range(4):
        cols = slice(n * 256, (n + 1) * 256)
        xh_ref[:, cols], xl_ref[:, cols] = split(x[:, cols] - dot(col[...], rhs[:, cols]))

    def weight_args(side):
        return (
            weights_out, weights_in.at[1 - side], w_send.at[side], w_recv.at[1 - side],
            ((left, right)[side], g),
        )

    weights_out[...] = jnp.concatenate([weights, jnp.zeros((8, BW - n_grp * 8), F32)], 1)
    for side in range(2):
        start(*weight_args(side))

    def amounts(e):
        avg_end(e)
        part = [
            dot_hi(w, avg[e, side].reshape(n_grp * 8, BW), ((1,), (0,))) * (1.0 / ROOT)
            for side, w in enumerate(weight_sides)
        ]
        return part[0], part[0] + part[1] + part[2]

    def expand(tile):
        return dot_hi(tile[:, :R], blocks, ((0,), (0,)))

    right_side = exchange_end(4)
    weighted = 0.5 * right_side
    mean = averages(weighted)
    avg_begin(0, mean)

    local_z = 0.5 * product(weighted, xh_ref, xl_ref)
    exchange_start(0, local_z)
    for side in range(2):
        wait(*weight_args(side))
    swapped = [pltpu.roll(weights_in[side], 4, 0)[:, : n_grp * 8] for side in range(2)]
    upper = lax.broadcasted_iota(jnp.int32, (8, n_grp * 8), 0) < 4
    weight_sides = [
        weights,
        jnp.where(upper, swapped[0], 0.0),
        jnp.where(upper, 0.0, swapped[1]),
    ]
    own, both = amounts(0)
    rz = sums_of(right_side, local_z) + ROOT * jnp.sum(own * mean, axis=0, keepdims=True)
    coarse_z = 0.5 * expand(both)
    z = exchange_end(0) + coarse_z

    prod = product(z, ah_ref, al_ref)
    exchange_start(1, prod)
    dp = sums_of(z, prod)
    gx_begin(0, jnp.where(sub == 0, rz, dp))
    image = exchange_end(1)

    half = 0.5 * image
    mean_q = averages(half)
    avg_begin(1, mean_q)
    local_q = 0.5 * product(half, xh_ref, xl_ref)
    exchange_start(2, local_q)
    z_begin(0, gx_total(0))
    own_q, both_q = amounts(1)
    coarse_q = 0.5 * expand(both_q)
    q = exchange_end(2) + coarse_q
    first = z_total(0)
    valid = lax.broadcasted_iota(jnp.int32, (1, BW), 1) < R
    rz0 = first[0:1]
    dp0 = first[1:2]
    alpha0 = rz0 / jnp.where(valid, dp0, 1.0)
    alpha0_rows = per_row(alpha0)
    z1 = z - alpha0_rows * q

    prod1 = product(z1, ah_ref, al_ref)
    exchange_start(3, prod1)
    residual = right_side - alpha0_rows * image
    rz = sums_of(residual, local_z - alpha0_rows * local_q) + ROOT * jnp.sum(
        (own - alpha0 * own_q) * (mean - alpha0 * mean_q), axis=0, keepdims=True
    )
    zz = sums_of(z1, prod1)
    zd = sums_of(z1, prod)
    gx_begin(1, jnp.where(sub == 0, rz, jnp.where(sub == 1, zz, zd)))
    z_begin(1, gx_total(1))
    image1 = exchange_end(3)
    last = z_total(1)
    rz1 = last[0:1]
    beta = rz1 / jnp.where(valid, rz0, 1.0)
    energy = last[1:2] + 2.0 * beta * last[2:3] + beta * beta * dp0
    alpha1 = rz1 / jnp.where(valid, energy, 1.0)
    alpha1_rows = per_row(alpha1)
    beta_rows = per_row(beta)
    sol_ref[...] = alpha0_rows * z + alpha1_rows * (z1 + beta_rows * z)
    res_ref[...] = residual - alpha1_rows * (image1 + beta_rows * image)
    for copy in started:
        copy.wait_send()


def iterate(n_grp, n_sub, *args):
    n_z = n_sub // X_DIM
    n_gx = n_grp * X_DIM
    out = jax.ShapeDtypeStruct((R, M), F32)
    dma = pltpu.SemaphoreType.DMA
    return pl.pallas_call(
        iterate_kernel,
        out_shape=(out, out),
        in_specs=[vmem()] * len(args),
        out_specs=(vmem(), vmem()),
        scratch_shapes=[
            pltpu.VMEM((M, M), BF16),
            pltpu.VMEM((M, M), BF16),
            pltpu.VMEM((M, M), F32),
            pltpu.VMEM((M, 4 * BW), BF16),
            pltpu.VMEM((4 * BW, M), BF16),
            pltpu.VMEM((BW, M), F32),
            pltpu.VMEM((BW, BW), F32),
            pltpu.VMEM((BW, BW), F32),
            pltpu.VMEM((5, 2, R, M // 2), F32),
            pltpu.VMEM((5, 2, R, M // 2), F32),
            pltpu.VMEM((n_grp, 8, BW), F32),
            pltpu.VMEM((2, 3, n_grp, 8, BW), F32),
            pltpu.VMEM((8, BW), F32),
            pltpu.VMEM((2, 8, BW), F32),
            pltpu.VMEM((2, n_gx, 8, BW), F32),
            pltpu.VMEM((2, n_z, 8, BW), F32),
            dma((5, 2)),
            dma((5, 2)),
            dma((n_grp,)),
            dma((n_grp,)),
            dma((2, 3, n_grp)),
            dma((2, 3, n_grp)),
            dma((2,)),
            dma((2,)),
            dma((2, n_gx)),
            dma((2, n_gx)),
            dma((2, n_z)),
            dma((2, n_z)),
        ],
        compiler_params=pltpu.CompilerParams(
            collective_id=0, has_side_effects=True, vmem_limit_bytes=40 * MIB
        ),
        cost_estimate=pl.CostEstimate(
            flops=2_000_000_000, bytes_accessed=10 * MIB, transcendentals=0
        ),
        name="iterate",
    )(*args)


def body(schur, loads, block_map, primal_map, disk_mask):
    a_high, a_low, x, inv, pivot, face, tile = invert(
        block_map[0], primal_map[0], schur[0, 0], loads[0, 0], disk_mask[0]
    )
    sol, res = iterate(
        lax.axis_size("grp"), lax.axis_size("sub"), face, tile, a_high, a_low, x, inv, pivot
    )
    return sol[None, None], res[None, None]


def solution(mesh):
    in_specs = (
        P("sub", "grp", None, None),
        P("sub", "grp", None, None),
        P("sub", "grp", None),
        P("sub", "grp", None),
        P("sub", "grp", None),
    )
    out_specs = (P("sub", "grp", None, None), P("sub", "grp", None, None))
    return jax.shard_map(body, mesh=mesh, in_specs=in_specs, out_specs=out_specs, check_vma=False)
```

```python
import jax
import jax.numpy as jnp
from jax import lax
from jax.experimental import pallas as pl
from jax.experimental.pallas import tpu as pltpu
from jax.sharding import PartitionSpec as P

F32 = jnp.float32
BF16 = jnp.bfloat16
HI = lax.Precision.HIGHEST
MESH = pl.DeviceIdType.MESH
M = 1024
R = 64
BW = 128
NB = 8
C = 32
X_DIM = 4
FIRST = NB - 4
ROOT = BW ** 0.5
LOWEST = -3e38
MIB = 1 << 20


def vmem():
    return pl.BlockSpec(memory_space=pltpu.VMEM)


def smem():
    return pl.BlockSpec(memory_space=pltpu.SMEM)


def split(value):
    high = value.astype(BF16)
    low = (value - high.astype(F32)).astype(BF16)
    return high, low


def dot(a, b):
    return jnp.dot(a, b, preferred_element_type=F32)


def dot_hi(a, b, dims):
    return lax.dot_general(a, b, (dims, ((), ())), precision=HI, preferred_element_type=F32)


def spread(v):
    return jnp.broadcast_to(v, (8, BW))


def column_inverse(c, sub):
    for j in range(0, 8, 2):
        at_a, at_b = sub == j, sub == j + 1
        fa, fb = c[j], c[j + 1]
        a = spread(fa[j : j + 1, :])
        b = spread(fb[j : j + 1, :])
        e = spread(fb[j + 1 : j + 2, :])
        det = a * e - b * b
        r1 = pltpu.reciprocal(det, approx=True)
        t = 2.0 - det * r1
        r = r1 * t
        new = []
        for l in range(8):
            if l == j:
                v = fa * e - fb * b
                new.append(jnp.where(at_a, e * r, jnp.where(at_b, -(b * r), -(v * r))))
            elif l == j + 1:
                v = fb * a - fa * b
                new.append(jnp.where(at_a, -(b * r), jnp.where(at_b, a * r, -(v * r))))
            else:
                ra = spread(c[l][j : j + 1, :])
                rb = spread(c[l][j + 1 : j + 2, :])
                ua = e * ra - b * rb
                ub = a * rb - b * ra
                v = fa * ua + fb * ub
                rest = c[l] - (v * r1) * t
                new.append(jnp.where(at_a, ua * r, jnp.where(at_b, ub * r, rest)))
        c = new
    return c


def dense_inverse(x, n, beside=()):
    beside = list(beside)
    groups = n // 8
    xs = [x[8 * i : 8 * i + 8, :] for i in range(groups)]
    lane = lax.broadcasted_iota(jnp.int32, (8, BW), 1)
    sub = lax.broadcasted_iota(jnp.int32, (8, BW), 0)
    for q in range(groups):
        k = 8 * q
        others = [(q + 1 + i) % groups for i in range(groups - 1)]
        own = [jnp.maximum(spread(xs[q][:, k + j : k + j + 1]), LOWEST) for j in range(8)]
        cols = {i: [spread(xs[i][:, k + j : k + j + 1]) for j in range(8)] for i in others}
        pivots = (lane >= k) & (lane < k + 8)
        r = column_inverse(own, sub)
        rows = [
            jnp.where(pivots, (lane == k + j).astype(F32), spread(xs[q][j : j + 1, :]))
            for j in range(8)
        ]
        p = r[0] * rows[0]
        for j in range(1, 8):
            p = p + r[j] * rows[j]
        lines = [spread(p[j : j + 1, :]) for j in range(8)]
        new = [None] * groups
        new[q] = p
        for i in others:
            y = jnp.where(pivots, 0.0, xs[i])
            for j in range(8):
                y = y - cols[i][j] * lines[j]
            new[i] = y
        xs = new
        if beside:
            beside.pop(0)()
    for work in beside:
        work()
    return jnp.concatenate(xs, 0)


def face_sources(bm_ref):
    places = [bm_ref[0, j] for j in range(NB)]
    out = []
    for f in range(NB):
        where = jnp.int32(0)
        for j in range(NB):
            where = where + jnp.where(places[j] == f, jnp.int32(j), jnp.int32(0))
        out.append(where)
    return out


def at(k):
    return pl.ds(pl.multiple_of(k * BW, BW), BW)


def four(value, axis):
    high, low = split(value)
    parts = [high, low, high, low] if axis == 1 else [high, high, low, low]
    return jnp.concatenate(parts, axis)


def elimination(x, col, rhs, panel, inv, here):
    def rows():
        panel[...] = dot(four(inv[...], 1), four(x[here, :], 0))
        col[...] = four(x[:, here], 1)
        x[:, here] = jnp.zeros((x.shape[0], BW), F32)
        rhs[...] = four(panel[...], 0)
        rhs[:, here] = four(inv[...], 0)

    def block(n):
        cols = slice(n * 256, (n + 1) * 256)

        def work():
            x[:, cols] = x[:, cols] - dot(col[...], rhs[:, cols])

        return work

    def finish():
        x[here, :] = panel[...]
        x[here, here] = inv[...]

    return rows, [block(n) for n in range(4)], finish


def nothing():
    pass


def next_pivot(x, inv, pivot, inverse, here, after):
    inv[...] = inverse
    p = dot(four(inverse, 1), four(x[here, after], 0))
    pivot[...] = x[after, after] - dot(four(x[after, here], 1), four(p, 0))


def pivot_step(x, col, rhs, panel, inv, pivot, last, here, after):
    rows, blocks, finish = elimination(x, col, rhs, panel, inv, last)
    rows()
    work = []
    for block in blocks:
        work += [block, nothing, nothing]
    inverse = dense_inverse(pivot[...], BW, work)
    finish()
    if after is None:
        inv[...] = inverse
    else:
        next_pivot(x, inv, pivot, inverse, here, after)


def invert_kernel(
    bm_ref, pm_ref, schur_ref, loads_ref, mask_ref,
    ah_ref, al_ref, x, inv, pivot, face_ref, tile_ref,
    col, rhs, panel, sums,
):
    source = face_sources(bm_ref)
    eye = lax.broadcasted_iota(jnp.int32, (BW, BW), 0) == lax.broadcasted_iota(
        jnp.int32, (BW, BW), 1
    )

    def load(f, h):
        row_at = pl.multiple_of(source[f] * BW, BW)
        col_at = pl.multiple_of(source[h] * BW, BW)
        block = schur_ref[pl.ds(row_at, BW), pl.ds(col_at, BW)]
        if f == h:
            penalty = 0.1 * mask_ref[:, pl.ds(col_at, BW)].astype(F32)
            block = block + jnp.where(eye, penalty, 0.0)
        return block

    def place(f):
        def work():
            rows = slice(f * BW, (f + 1) * BW)
            at_f = pl.multiple_of(source[f] * BW, BW)
            face_ref[:, rows] = loads_ref[:, pl.ds(at_f, BW)]
            for h in range(NB):
                cols = slice(h * BW, (h + 1) * BW)
                block = load(f, h)
                x[rows, cols] = block
                sums[f : f + 1, cols] = jnp.sum(block, axis=0, keepdims=True)
                ah_ref[rows, cols], al_ref[rows, cols] = split(block)

        return work

    first = slice(0, BW)
    inverse = dense_inverse(load(0, 0), BW, [place(f) for f in range(NB)])
    next_pivot(x, inv, pivot, inverse, first, slice(BW, 2 * BW))

    sub = lax.broadcasted_iota(jnp.int32, (8, BW), 0)
    lane = lax.broadcasted_iota(jnp.int32, (8, BW), 1)
    primal = jnp.zeros((8, BW), F32)
    shifted = jnp.zeros((8, BW), F32)
    for f in range(NB):
        coarse = pm_ref[0, source[f]]
        primal = jnp.where((sub == f) & (lane == coarse), 1.0, primal)
        shifted = jnp.where((sub == f) & (lane == coarse + C), 1.0, shifted)
    block_sums = dot_hi(sums[...], block_indicator(), ((1,), (1,))) / BW
    tile_ref[...] = dot_hi(block_sums, primal, ((1,), (0,))) + shifted

    def step(k, carry):
        pivot_step(x, col, rhs, panel, inv, pivot, at(k - 1), at(k), at(k + 1))
        return carry

    lax.fori_loop(1, FIRST, step, 0)


def invert(block_map, primal_map, schur, loads, mask):
    def arr(shape, dtype=F32):
        return jax.ShapeDtypeStruct(shape, dtype)

    return pl.pallas_call(
        invert_kernel,
        out_shape=(
            arr((M, M), BF16), arr((M, M), BF16), arr((M, M)), arr((BW, BW)),
            arr((BW, BW)), arr((R, M)), arr((8, BW)),
        ),
        in_specs=[smem(), smem(), vmem(), vmem(), vmem()],
        out_specs=(vmem(),) * 7,
        scratch_shapes=[
            pltpu.VMEM((M, 4 * BW), BF16),
            pltpu.VMEM((4 * BW, M), BF16),
            pltpu.VMEM((BW, M), F32),
            pltpu.VMEM((8, M), F32),
        ],
        compiler_params=pltpu.CompilerParams(vmem_limit_bytes=40 * MIB),
        cost_estimate=pl.CostEstimate(
            flops=20_000_000_000, bytes_accessed=12 * MIB, transcendentals=0
        ),
        name="invert",
    )(block_map, primal_map, schur, loads, mask)


def block_indicator():
    return (
        lax.broadcasted_iota(jnp.int32, (8, M), 1) // BW
        == lax.broadcasted_iota(jnp.int32, (8, M), 0)
    ).astype(F32)


def product(value, high_ref, low_ref):
    high, low = split(value)
    both = dot(jnp.concatenate([high, low], 0), high_ref[...])
    return both[:R] + both[R:] + dot(high, low_ref[...])


def iterate_kernel(
    loads_ref, tile_ref, ah_ref, al_ref, x_ref, inv_ref, pivot_ref,
    sol_ref, res_ref,
    xh_ref, xl_ref, x, col, rhs, panel, inv, pivot,
    face_out, face_in, tiles, avg, weights_out, weights_in, sum_gx, sum_z,
    face_send, face_recv, tile_send, tile_recv, avg_send, avg_recv, w_send, w_recv,
    gx_send, gx_recv, z_send, z_recv,
):
    s = lax.axis_index("sub")
    g = lax.axis_index("grp")
    n_sub = lax.axis_size("sub")
    n_grp = lax.axis_size("grp")
    n_z = n_sub // X_DIM
    n_gx = n_grp * X_DIM
    xi = lax.rem(s, X_DIM)
    zi = s // X_DIM
    left = lax.rem(s + n_sub - 1, n_sub)
    right = lax.rem(s + 1, n_sub)
    mine = xi * n_grp + g

    def around(d):
        return lax.rem(g + d, n_grp)

    def gx_peer(d):
        return (zi * X_DIM + lax.rem(xi + d // n_grp, X_DIM), around(d % n_grp))

    def gx_slot(d):
        return lax.rem(xi + d // n_grp, X_DIM) * n_grp + around(d % n_grp)

    def z_peer(d):
        return (lax.rem(zi + d, n_z) * X_DIM + xi, g)

    partners = [(left, around(d)) for d in range(n_grp)]
    partners += [(right, around(d)) for d in range(n_grp)]
    partners += [gx_peer(d) for d in range(1, n_gx)]
    partners += [z_peer(d) for d in range(1, n_z)]
    barrier = pltpu.get_barrier_semaphore()
    for partner in partners:
        pl.semaphore_signal(barrier, inc=1, device_id=partner, device_id_type=MESH)

    started = []

    def copy_of(src, dst, send, recv, target):
        return pltpu.make_async_remote_copy(
            src_ref=src, dst_ref=dst, send_sem=send, recv_sem=recv,
            device_id=target, device_id_type=MESH,
        )

    def start(*args):
        copy = copy_of(*args)
        copy.start()
        started.append(copy)

    def wait(*args):
        copy_of(*args).wait_recv()

    def gx_begin(e, tile):
        sum_gx[e, mine] = tile
        for d in range(1, n_gx):
            start(
                sum_gx.at[e, mine], sum_gx.at[e, mine],
                gx_send.at[e, d], gx_recv.at[e, mine], gx_peer(d),
            )

    def gx_total(e):
        for d in range(1, n_gx):
            o = gx_slot(d)
            wait(sum_gx.at[e, o], sum_gx.at[e, o], gx_send.at[e, d], gx_recv.at[e, o], gx_peer(d))
        return jnp.sum(sum_gx[e], axis=0)

    def z_begin(e, tile):
        sum_z[e, zi] = tile
        for d in range(1, n_z):
            start(
                sum_z.at[e, zi], sum_z.at[e, zi], z_send.at[e, d], z_recv.at[e, zi], z_peer(d)
            )

    def z_total(e):
        for d in range(1, n_z):
            o = lax.rem(zi + d, n_z)
            wait(sum_z.at[e, o], sum_z.at[e, o], z_send.at[e, d], z_recv.at[e, o], z_peer(d))
        return jnp.sum(sum_z[e], axis=0)

    def avg_begin(e, tile):
        avg[e, 0, g] = tile
        for d in range(1, n_grp):
            start(
                avg.at[e, 0, g], avg.at[e, 0, g],
                avg_send.at[e, 0, d], avg_recv.at[e, 0, g], (s, around(d)),
            )
        for side, target in ((1, right), (2, left)):
            for d in range(n_grp):
                start(
                    avg.at[e, 0, g], avg.at[e, side, g],
                    avg_send.at[e, side, d], avg_recv.at[e, side, g], (target, around(d)),
                )

    def avg_end(e):
        for side, target in ((0, s), (1, right), (2, left)):
            for d in range(0 if side else 1, n_grp):
                o = around(d)
                wait(
                    avg.at[e, side, o], avg.at[e, side, o],
                    avg_send.at[e, side, d], avg_recv.at[e, side, o], (target, o),
                )

    def face_args(e, side):
        return (
            face_out.at[e, side], face_in.at[e, 1 - side],
            face_send.at[e, side], face_recv.at[e, 1 - side],
            ((left, right)[side], g),
        )

    def exchange_start(e, value):
        face_out[e, 0] = value[:, : M // 2]
        face_out[e, 1] = value[:, M // 2 :]
        for side in range(2):
            start(*face_args(e, side))

    def exchange_end(e):
        for side in range(2):
            wait(*face_args(e, side))
        first = face_out[e, 0] + face_in[e, 0]
        second = face_out[e, 1] + face_in[e, 1]
        return jnp.concatenate([first, second], 1)

    blocks = block_indicator()
    sub = lax.broadcasted_iota(jnp.int32, (8, BW), 0)
    ones = jnp.ones((8, M), F32)
    pad = jnp.zeros((8, BW - R), F32)

    def averages(w):
        t = dot_hi(blocks, w, ((1,), (1,))) * (1.0 / ROOT)
        return jnp.concatenate([t, pad], 1)

    def sums_of(u, v):
        t = dot_hi(ones, u * v, ((1,), (1,)))
        return jnp.concatenate([t, pad], 1)

    def per_row(line):
        tile = jnp.where(sub == 0, jnp.broadcast_to(line, (8, BW)), 0.0)
        wide = dot_hi(tile, jnp.ones((8, BW), F32), ((0,), (0,)))[:R]
        return jnp.concatenate([wide] * NB, 1)

    def weight_args(side):
        return (
            weights_out, weights_in.at[1 - side], w_send.at[side], w_recv.at[1 - side],
            ((left, right)[side], g),
        )

    def piece(k):
        return slice(k * BW, (k + 1) * BW)

    x[...] = x_ref[...]
    inv[...] = inv_ref[...]
    pivot[...] = pivot_ref[...]
    pivot_step(
        x, col, rhs, panel, inv, pivot, piece(FIRST - 1), piece(FIRST), piece(FIRST + 1)
    )
    pl.semaphore_wait(barrier, len(partners))
    tiles[g] = tile_ref[...]
    for d in range(1, n_grp):
        start(tiles.at[g], tiles.at[g], tile_send.at[d], tile_recv.at[g], (s, around(d)))
    exchange_start(4, loads_ref[...])

    def step(k, carry):
        pivot_step(x, col, rhs, panel, inv, pivot, at(k - 1), at(k), at(k + 1))
        return carry

    lax.fori_loop(FIRST + 1, NB - 1, step, 0)
    right_side = exchange_end(4)
    weighted = 0.5 * right_side
    mean = averages(weighted)
    avg_begin(0, mean)

    for d in range(1, n_grp):
        o = around(d)
        wait(tiles.at[o], tiles.at[o], tile_send.at[d], tile_recv.at[o], (s, o))
    contributions = tiles[...].reshape(n_grp * 8, BW)
    primal_all = contributions[:, C : 2 * C]
    local_all = contributions[:, :C]
    coarse = dot_hi(primal_all, local_all, ((0,), (0,)))
    coarse = coarse + (
        lax.broadcasted_iota(jnp.int32, (C, C), 0) == lax.broadcasted_iota(jnp.int32, (C, C), 1)
    ).astype(F32)
    coarse_inverse = dense_inverse(
        jnp.concatenate([coarse, jnp.zeros((C, BW - C), F32)], 1), C
    )[:, :C]
    primal = tile_ref[:, C : 2 * C]
    weights = dot_hi(dot_hi(primal, coarse_inverse, ((1,), (0,))), primal_all, ((1,), (1,)))
    pivot_step(x, col, rhs, panel, inv, pivot, piece(NB - 2), piece(NB - 1), None)
    weights_out[...] = jnp.concatenate([weights, jnp.zeros((8, BW - n_grp * 8), F32)], 1)
    for side in range(2):
        start(*weight_args(side))
    rows, _, finish = elimination(x, col, rhs, panel, inv, piece(NB - 1))
    rows()
    finish()
    col[M - BW :, :] = jnp.zeros((BW, 4 * BW), BF16)
    for n in range(4):
        cols = slice(n * 256, (n + 1) * 256)
        xh_ref[:, cols], xl_ref[:, cols] = split(x[:, cols] - dot(col[...], rhs[:, cols]))

    def amounts(e):
        avg_end(e)
        part = [
            dot_hi(w, avg[e, side].reshape(n_grp * 8, BW), ((1,), (0,))) * (1.0 / ROOT)
            for side, w in enumerate(weight_sides)
        ]
        return part[0], part[0] + part[1] + part[2]

    def expand(tile):
        return dot_hi(tile[:, :R], blocks, ((0,), (0,)))

    local_z = 0.5 * product(weighted, xh_ref, xl_ref)
    exchange_start(0, local_z)
    for side in range(2):
        wait(*weight_args(side))
    swapped = [pltpu.roll(weights_in[side], 4, 0)[:, : n_grp * 8] for side in range(2)]
    upper = lax.broadcasted_iota(jnp.int32, (8, n_grp * 8), 0) < 4
    weight_sides = [
        weights,
        jnp.where(upper, swapped[0], 0.0),
        jnp.where(upper, 0.0, swapped[1]),
    ]
    own, both = amounts(0)
    rz = sums_of(right_side, local_z) + ROOT * jnp.sum(own * mean, axis=0, keepdims=True)
    coarse_z = 0.5 * expand(both)
    z = exchange_end(0) + coarse_z

    prod = product(z, ah_ref, al_ref)
    exchange_start(1, prod)
    dp = sums_of(z, prod)
    gx_begin(0, jnp.where(sub == 0, rz, dp))
    image = exchange_end(1)

    half = 0.5 * image
    mean_q = averages(half)
    avg_begin(1, mean_q)
    local_q = 0.5 * product(half, xh_ref, xl_ref)
    exchange_start(2, local_q)
    z_begin(0, gx_total(0))
    own_q, both_q = amounts(1)
    coarse_q = 0.5 * expand(both_q)
    q = exchange_end(2) + coarse_q
    first = z_total(0)
    valid = lax.broadcasted_iota(jnp.int32, (1, BW), 1) < R
    rz0 = first[0:1]
    dp0 = first[1:2]
    alpha0 = rz0 / jnp.where(valid, dp0, 1.0)
    alpha0_rows = per_row(alpha0)
    z1 = z - alpha0_rows * q

    prod1 = product(z1, ah_ref, al_ref)
    exchange_start(3, prod1)
    residual = right_side - alpha0_rows * image
    rz = sums_of(residual, local_z - alpha0_rows * local_q) + ROOT * jnp.sum(
        (own - alpha0 * own_q) * (mean - alpha0 * mean_q), axis=0, keepdims=True
    )
    zz = sums_of(z1, prod1)
    zd = sums_of(z1, prod)
    gx_begin(1, jnp.where(sub == 0, rz, jnp.where(sub == 1, zz, zd)))
    z_begin(1, gx_total(1))
    image1 = exchange_end(3)
    last = z_total(1)
    rz1 = last[0:1]
    beta = rz1 / jnp.where(valid, rz0, 1.0)
    energy = last[1:2] + 2.0 * beta * last[2:3] + beta * beta * dp0
    alpha1 = rz1 / jnp.where(valid, energy, 1.0)
    alpha1_rows = per_row(alpha1)
    beta_rows = per_row(beta)
    sol_ref[...] = alpha0_rows * z + alpha1_rows * (z1 + beta_rows * z)
    res_ref[...] = residual - alpha1_rows * (image1 + beta_rows * image)
    for copy in started:
        copy.wait_send()


def iterate(n_grp, n_sub, *args):
    n_z = n_sub // X_DIM
    n_gx = n_grp * X_DIM
    out = jax.ShapeDtypeStruct((R, M), F32)
    dma = pltpu.SemaphoreType.DMA
    return pl.pallas_call(
        iterate_kernel,
        out_shape=(out, out),
        in_specs=[vmem()] * len(args),
        out_specs=(vmem(), vmem()),
        scratch_shapes=[
            pltpu.VMEM((M, M), BF16),
            pltpu.VMEM((M, M), BF16),
            pltpu.VMEM((M, M), F32),
            pltpu.VMEM((M, 4 * BW), BF16),
            pltpu.VMEM((4 * BW, M), BF16),
            pltpu.VMEM((BW, M), F32),
            pltpu.VMEM((BW, BW), F32),
            pltpu.VMEM((BW, BW), F32),
            pltpu.VMEM((5, 2, R, M // 2), F32),
            pltpu.VMEM((5, 2, R, M // 2), F32),
            pltpu.VMEM((n_grp, 8, BW), F32),
            pltpu.VMEM((2, 3, n_grp, 8, BW), F32),
            pltpu.VMEM((8, BW), F32),
            pltpu.VMEM((2, 8, BW), F32),
            pltpu.VMEM((2, n_gx, 8, BW), F32),
            pltpu.VMEM((2, n_z, 8, BW), F32),
            dma((5, 2)),
            dma((5, 2)),
            dma((n_grp,)),
            dma((n_grp,)),
            dma((2, 3, n_grp)),
            dma((2, 3, n_grp)),
            dma((2,)),
            dma((2,)),
            dma((2, n_gx)),
            dma((2, n_gx)),
            dma((2, n_z)),
            dma((2, n_z)),
        ],
        compiler_params=pltpu.CompilerParams(
            collective_id=0, has_side_effects=True, vmem_limit_bytes=40 * MIB
        ),
        cost_estimate=pl.CostEstimate(
            flops=2_000_000_000, bytes_accessed=10 * MIB, transcendentals=0
        ),
        name="iterate",
    )(*args)


def body(schur, loads, block_map, primal_map, disk_mask):
    a_high, a_low, x, inv, pivot, face, tile = invert(
        block_map[0], primal_map[0], schur[0, 0], loads[0, 0], disk_mask[0]
    )
    sol, res = iterate(
        lax.axis_size("grp"), lax.axis_size("sub"), face, tile, a_high, a_low, x, inv, pivot
    )
    return sol[None, None], res[None, None]


def solution(mesh):
    in_specs = (
        P("sub", "grp", None, None),
        P("sub", "grp", None, None),
        P("sub", "grp", None),
        P("sub", "grp", None),
        P("sub", "grp", None),
    )
    out_specs = (P("sub", "grp", None, None), P("sub", "grp", None, None))
    return jax.shard_map(body, mesh=mesh, in_specs=in_specs, out_specs=out_specs, check_vma=False)
```

```python
import jax
import jax.numpy as jnp
from jax import lax
from jax.experimental import pallas as pl
from jax.experimental.pallas import tpu as pltpu
from jax.sharding import PartitionSpec as P

F32 = jnp.float32
BF16 = jnp.bfloat16
HI = lax.Precision.HIGHEST
MESH = pl.DeviceIdType.MESH
M = 1024
R = 64
BW = 128
NB = 8
C = 32
X_DIM = 4
FIRST = NB - 4
ROOT = BW ** 0.5
LOWEST = -3e38
MIB = 1 << 20


def vmem():
    return pl.BlockSpec(memory_space=pltpu.VMEM)


def smem():
    return pl.BlockSpec(memory_space=pltpu.SMEM)


def split(value):
    high = value.astype(BF16)
    low = (value - high.astype(F32)).astype(BF16)
    return high, low


def dot(a, b):
    return jnp.dot(a, b, preferred_element_type=F32)


def dot_hi(a, b, dims):
    return lax.dot_general(a, b, (dims, ((), ())), precision=HI, preferred_element_type=F32)


def spread(v):
    return jnp.broadcast_to(v, (8, BW))


def column_inverse(c, sub):
    for j in range(0, 8, 2):
        at_a, at_b = sub == j, sub == j + 1
        fa, fb = c[j], c[j + 1]
        a = spread(fa[j : j + 1, :])
        b = spread(fb[j : j + 1, :])
        e = spread(fb[j + 1 : j + 2, :])
        det = a * e - b * b
        r1 = pltpu.reciprocal(det, approx=True)
        t = 2.0 - det * r1
        r = r1 * t
        new = []
        for l in range(8):
            if l == j:
                v = fa * e - fb * b
                new.append(jnp.where(at_a, e * r, jnp.where(at_b, -(b * r), -(v * r))))
            elif l == j + 1:
                v = fb * a - fa * b
                new.append(jnp.where(at_a, -(b * r), jnp.where(at_b, a * r, -(v * r))))
            else:
                ra = spread(c[l][j : j + 1, :])
                rb = spread(c[l][j + 1 : j + 2, :])
                ua = e * ra - b * rb
                ub = a * rb - b * ra
                v = fa * ua + fb * ub
                rest = c[l] - (v * r1) * t
                new.append(jnp.where(at_a, ua * r, jnp.where(at_b, ub * r, rest)))
        c = new
    return c


def dense_inverse(x, n, beside=()):
    beside = list(beside)
    groups = n // 8
    xs = [x[8 * i : 8 * i + 8, :] for i in range(groups)]
    lane = lax.broadcasted_iota(jnp.int32, (8, BW), 1)
    sub = lax.broadcasted_iota(jnp.int32, (8, BW), 0)
    for q in range(groups):
        k = 8 * q
        others = [(q + 1 + i) % groups for i in range(groups - 1)]
        own = [jnp.maximum(spread(xs[q][:, k + j : k + j + 1]), LOWEST) for j in range(8)]
        cols = {i: [spread(xs[i][:, k + j : k + j + 1]) for j in range(8)] for i in others}
        pivots = (lane >= k) & (lane < k + 8)
        r = column_inverse(own, sub)
        rows = [
            jnp.where(pivots, (lane == k + j).astype(F32), spread(xs[q][j : j + 1, :]))
            for j in range(8)
        ]
        p = r[0] * rows[0]
        for j in range(1, 8):
            p = p + r[j] * rows[j]
        lines = [spread(p[j : j + 1, :]) for j in range(8)]
        new = [None] * groups
        new[q] = p
        for i in others:
            y = jnp.where(pivots, 0.0, xs[i])
            for j in range(8):
                y = y - cols[i][j] * lines[j]
            new[i] = y
        xs = new
        if beside:
            beside.pop(0)()
    for work in beside:
        work()
    return jnp.concatenate(xs, 0)


def face_sources(bm_ref):
    places = [bm_ref[0, j] for j in range(NB)]
    out = []
    for f in range(NB):
        where = jnp.int32(0)
        for j in range(NB):
            where = where + jnp.where(places[j] == f, jnp.int32(j), jnp.int32(0))
        out.append(where)
    return out


def at(k):
    return pl.ds(pl.multiple_of(k * BW, BW), BW)


def four(value, axis):
    high, low = split(value)
    parts = [high, low, high, low] if axis == 1 else [high, high, low, low]
    return jnp.concatenate(parts, axis)


def elimination(x, col, rhs, panel, inv, here):
    def rows():
        panel[...] = dot(four(inv[...], 1), four(x[here, :], 0))
        col[...] = four(x[:, here], 1)
        x[:, here] = jnp.zeros((x.shape[0], BW), F32)
        rhs[...] = four(panel[...], 0)
        rhs[:, here] = four(inv[...], 0)

    def block(n):
        cols = slice(n * 256, (n + 1) * 256)

        def work():
            x[:, cols] = x[:, cols] - dot(col[...], rhs[:, cols])

        return work

    def finish():
        x[here, :] = panel[...]
        x[here, here] = inv[...]

    return rows, [block(n) for n in range(4)], finish


def nothing():
    pass


def next_pivot(x, inv, pivot, inverse, here, after):
    inv[...] = inverse
    p = dot(four(inverse, 1), four(x[here, after], 0))
    pivot[...] = x[after, after] - dot(four(x[after, here], 1), four(p, 0))


def pivot_step(x, col, rhs, panel, inv, pivot, last, here, after):
    rows, blocks, finish = elimination(x, col, rhs, panel, inv, last)
    rows()
    work = []
    for block in blocks:
        work += [block, nothing, nothing]
    inverse = dense_inverse(pivot[...], BW, work)
    finish()
    if after is None:
        inv[...] = inverse
    else:
        next_pivot(x, inv, pivot, inverse, here, after)


def invert_kernel(
    bm_ref, pm_ref, schur_ref, loads_ref, mask_ref,
    ah_ref, al_ref, x, inv, pivot, face_ref, tile_ref,
    col, rhs, panel, sums,
):
    source = face_sources(bm_ref)
    eye = lax.broadcasted_iota(jnp.int32, (BW, BW), 0) == lax.broadcasted_iota(
        jnp.int32, (BW, BW), 1
    )

    def load(f, h):
        row_at = pl.multiple_of(source[f] * BW, BW)
        col_at = pl.multiple_of(source[h] * BW, BW)
        block = schur_ref[pl.ds(row_at, BW), pl.ds(col_at, BW)]
        if f == h:
            penalty = 0.1 * mask_ref[:, pl.ds(col_at, BW)].astype(F32)
            block = block + jnp.where(eye, penalty, 0.0)
        return block

    def place(f):
        def work():
            rows = slice(f * BW, (f + 1) * BW)
            at_f = pl.multiple_of(source[f] * BW, BW)
            face_ref[:, rows] = loads_ref[:, pl.ds(at_f, BW)]
            for h in range(NB):
                cols = slice(h * BW, (h + 1) * BW)
                block = load(f, h)
                x[rows, cols] = block
                sums[f : f + 1, cols] = jnp.sum(block, axis=0, keepdims=True)
                ah_ref[rows, cols], al_ref[rows, cols] = split(block)

        return work

    first = slice(0, BW)
    inverse = dense_inverse(load(0, 0), BW, [place(f) for f in range(NB)])
    next_pivot(x, inv, pivot, inverse, first, slice(BW, 2 * BW))

    sub = lax.broadcasted_iota(jnp.int32, (8, BW), 0)
    lane = lax.broadcasted_iota(jnp.int32, (8, BW), 1)
    primal = jnp.zeros((8, BW), F32)
    shifted = jnp.zeros((8, BW), F32)
    for f in range(NB):
        coarse = pm_ref[0, source[f]]
        primal = jnp.where((sub == f) & (lane == coarse), 1.0, primal)
        shifted = jnp.where((sub == f) & (lane == coarse + C), 1.0, shifted)
    block_sums = dot_hi(sums[...], block_indicator(), ((1,), (1,))) / BW
    tile_ref[...] = dot_hi(block_sums, primal, ((1,), (0,))) + shifted

    def step(k, carry):
        pivot_step(x, col, rhs, panel, inv, pivot, at(k - 1), at(k), at(k + 1))
        return carry

    lax.fori_loop(1, FIRST, step, 0)


def invert(block_map, primal_map, schur, loads, mask):
    def arr(shape, dtype=F32):
        return jax.ShapeDtypeStruct(shape, dtype)

    return pl.pallas_call(
        invert_kernel,
        out_shape=(
            arr((M, M), BF16), arr((M, M), BF16), arr((M, M)), arr((BW, BW)),
            arr((BW, BW)), arr((R, M)), arr((8, BW)),
        ),
        in_specs=[smem(), smem(), vmem(), vmem(), vmem()],
        out_specs=(vmem(),) * 7,
        scratch_shapes=[
            pltpu.VMEM((M, 4 * BW), BF16),
            pltpu.VMEM((4 * BW, M), BF16),
            pltpu.VMEM((BW, M), F32),
            pltpu.VMEM((8, M), F32),
        ],
        compiler_params=pltpu.CompilerParams(vmem_limit_bytes=40 * MIB),
        cost_estimate=pl.CostEstimate(
            flops=20_000_000_000, bytes_accessed=12 * MIB, transcendentals=0
        ),
        name="invert",
    )(block_map, primal_map, schur, loads, mask)


def block_indicator():
    return (
        lax.broadcasted_iota(jnp.int32, (8, M), 1) // BW
        == lax.broadcasted_iota(jnp.int32, (8, M), 0)
    ).astype(F32)


def product(value, high_ref, low_ref):
    high, low = split(value)
    both = dot(jnp.concatenate([high, low], 0), high_ref[...])
    return both[:R] + both[R:] + dot(high, low_ref[...])


def iterate_kernel(
    loads_ref, tile_ref, ah_ref, al_ref, x_ref, inv_ref, pivot_ref,
    sol_ref, res_ref,
    xh_ref, xl_ref, x, col, rhs, panel, inv, pivot,
    face_out, face_in, tiles, avg, weights_out, weights_in, sum_gx, sum_z,
    face_send, face_recv, tile_send, tile_recv, avg_send, avg_recv, w_send, w_recv,
    gx_send, gx_recv, z_send, z_recv,
):
    s = lax.axis_index("sub")
    g = lax.axis_index("grp")
    n_sub = lax.axis_size("sub")
    n_grp = lax.axis_size("grp")
    n_z = n_sub // X_DIM
    n_gx = n_grp * X_DIM
    xi = lax.rem(s, X_DIM)
    zi = s // X_DIM
    left = lax.rem(s + n_sub - 1, n_sub)
    right = lax.rem(s + 1, n_sub)
    mine = xi * n_grp + g

    def around(d):
        return lax.rem(g + d, n_grp)

    def gx_peer(d):
        return (zi * X_DIM + lax.rem(xi + d // n_grp, X_DIM), around(d % n_grp))

    def gx_slot(d):
        return lax.rem(xi + d // n_grp, X_DIM) * n_grp + around(d % n_grp)

    def z_peer(d):
        return (lax.rem(zi + d, n_z) * X_DIM + xi, g)

    partners = [(left, around(d)) for d in range(n_grp)]
    partners += [(right, around(d)) for d in range(n_grp)]
    partners += [gx_peer(d) for d in range(1, n_gx)]
    partners += [z_peer(d) for d in range(1, n_z)]
    barrier = pltpu.get_barrier_semaphore()
    for partner in partners:
        pl.semaphore_signal(barrier, inc=1, device_id=partner, device_id_type=MESH)

    started = []

    def copy_of(src, dst, send, recv, target):
        return pltpu.make_async_remote_copy(
            src_ref=src, dst_ref=dst, send_sem=send, recv_sem=recv,
            device_id=target, device_id_type=MESH,
        )

    def start(*args):
        copy = copy_of(*args)
        copy.start()
        started.append(copy)

    def wait(*args):
        copy_of(*args).wait_recv()

    def gx_begin(e, tile):
        sum_gx[e, mine] = tile
        for d in range(1, n_gx):
            start(
                sum_gx.at[e, mine], sum_gx.at[e, mine],
                gx_send.at[e, d], gx_recv.at[e, mine], gx_peer(d),
            )

    def gx_total(e):
        for d in range(1, n_gx):
            o = gx_slot(d)
            wait(sum_gx.at[e, o], sum_gx.at[e, o], gx_send.at[e, d], gx_recv.at[e, o], gx_peer(d))
        return jnp.sum(sum_gx[e], axis=0)

    def z_begin(e, tile):
        sum_z[e, zi] = tile
        for d in range(1, n_z):
            start(
                sum_z.at[e, zi], sum_z.at[e, zi], z_send.at[e, d], z_recv.at[e, zi], z_peer(d)
            )

    def z_total(e):
        for d in range(1, n_z):
            o = lax.rem(zi + d, n_z)
            wait(sum_z.at[e, o], sum_z.at[e, o], z_send.at[e, d], z_recv.at[e, o], z_peer(d))
        return jnp.sum(sum_z[e], axis=0)

    def avg_begin(e, tile):
        avg[e, 0, g] = tile
        for d in range(1, n_grp):
            start(
                avg.at[e, 0, g], avg.at[e, 0, g],
                avg_send.at[e, 0, d], avg_recv.at[e, 0, g], (s, around(d)),
            )
        for side, target in ((1, right), (2, left)):
            for d in range(n_grp):
                start(
                    avg.at[e, 0, g], avg.at[e, side, g],
                    avg_send.at[e, side, d], avg_recv.at[e, side, g], (target, around(d)),
                )

    def avg_end(e):
        for side, target in ((0, s), (1, right), (2, left)):
            for d in range(0 if side else 1, n_grp):
                o = around(d)
                wait(
                    avg.at[e, side, o], avg.at[e, side, o],
                    avg_send.at[e, side, d], avg_recv.at[e, side, o], (target, o),
                )

    def face_args(e, side):
        return (
            face_out.at[e, side], face_in.at[e, 1 - side],
            face_send.at[e, side], face_recv.at[e, 1 - side],
            ((left, right)[side], g),
        )

    def exchange_start(e, value):
        face_out[e, 0] = value[:, : M // 2]
        face_out[e, 1] = value[:, M // 2 :]
        for side in range(2):
            start(*face_args(e, side))

    def exchange_end(e):
        for side in range(2):
            wait(*face_args(e, side))
        first = face_out[e, 0] + face_in[e, 0]
        second = face_out[e, 1] + face_in[e, 1]
        return jnp.concatenate([first, second], 1)

    blocks = block_indicator()
    sub = lax.broadcasted_iota(jnp.int32, (8, BW), 0)
    ones = jnp.ones((8, M), F32)
    pad = jnp.zeros((8, BW - R), F32)

    def averages(w):
        t = dot_hi(blocks, w, ((1,), (1,))) * (1.0 / ROOT)
        return jnp.concatenate([t, pad], 1)

    def sums_of(u, v):
        t = dot_hi(ones, u * v, ((1,), (1,)))
        return jnp.concatenate([t, pad], 1)

    def per_row(line):
        tile = jnp.where(sub == 0, jnp.broadcast_to(line, (8, BW)), 0.0)
        wide = dot_hi(tile, jnp.ones((8, BW), F32), ((0,), (0,)))[:R]
        return jnp.concatenate([wide] * NB, 1)

    def weight_args(side):
        return (
            weights_out, weights_in.at[1 - side], w_send.at[side], w_recv.at[1 - side],
            ((left, right)[side], g),
        )

    def piece(k):
        return slice(k * BW, (k + 1) * BW)

    x[...] = x_ref[...]
    inv[...] = inv_ref[...]
    pivot[...] = pivot_ref[...]
    pivot_step(
        x, col, rhs, panel, inv, pivot, piece(FIRST - 1), piece(FIRST), piece(FIRST + 1)
    )
    pl.semaphore_wait(barrier, len(partners))
    tiles[g] = tile_ref[...]
    for d in range(1, n_grp):
        start(tiles.at[g], tiles.at[g], tile_send.at[d], tile_recv.at[g], (s, around(d)))
    exchange_start(4, loads_ref[...])

    def step(k, carry):
        pivot_step(x, col, rhs, panel, inv, pivot, at(k - 1), at(k), at(k + 1))
        return carry

    lax.fori_loop(FIRST + 1, NB - 1, step, 0)
    right_side = exchange_end(4)
    weighted = 0.5 * right_side
    mean = averages(weighted)
    avg_begin(0, mean)

    for d in range(1, n_grp):
        o = around(d)
        wait(tiles.at[o], tiles.at[o], tile_send.at[d], tile_recv.at[o], (s, o))
    contributions = tiles[...].reshape(n_grp * 8, BW)
    primal_all = contributions[:, C : 2 * C]
    local_all = contributions[:, :C]
    coarse = dot_hi(primal_all, local_all, ((0,), (0,)))
    coarse = coarse + (
        lax.broadcasted_iota(jnp.int32, (C, C), 0) == lax.broadcasted_iota(jnp.int32, (C, C), 1)
    ).astype(F32)
    coarse_inverse = dense_inverse(
        jnp.concatenate([coarse, jnp.zeros((C, BW - C), F32)], 1), C
    )[:, :C]
    primal = tile_ref[:, C : 2 * C]
    weights = dot_hi(dot_hi(primal, coarse_inverse, ((1,), (0,))), primal_all, ((1,), (1,)))
    pivot_step(x, col, rhs, panel, inv, pivot, piece(NB - 2), piece(NB - 1), None)
    weights_out[...] = jnp.concatenate([weights, jnp.zeros((8, BW - n_grp * 8), F32)], 1)
    for side in range(2):
        start(*weight_args(side))
    rows, _, finish = elimination(x, col, rhs, panel, inv, piece(NB - 1))
    rows()
    finish()
    col[M - BW :, :] = jnp.zeros((BW, 4 * BW), BF16)
    for n in range(4):
        cols = slice(n * 256, (n + 1) * 256)
        xh_ref[:, cols], xl_ref[:, cols] = split(x[:, cols] - dot(col[...], rhs[:, cols]))

    def amounts(e):
        avg_end(e)
        part = [
            dot_hi(w, avg[e, side].reshape(n_grp * 8, BW), ((1,), (0,))) * (1.0 / ROOT)
            for side, w in enumerate(weight_sides)
        ]
        return part[0], part[0] + part[1] + part[2]

    def expand(tile):
        return dot_hi(tile[:, :R], blocks, ((0,), (0,)))

    local_z = 0.5 * product(weighted, xh_ref, xl_ref)
    exchange_start(0, local_z)
    for side in range(2):
        wait(*weight_args(side))
    swapped = [pltpu.roll(weights_in[side], 4, 0)[:, : n_grp * 8] for side in range(2)]
    upper = lax.broadcasted_iota(jnp.int32, (8, n_grp * 8), 0) < 4
    weight_sides = [
        weights,
        jnp.where(upper, swapped[0], 0.0),
        jnp.where(upper, 0.0, swapped[1]),
    ]
    own, both = amounts(0)
    rz = sums_of(right_side, local_z) + ROOT * jnp.sum(own * mean, axis=0, keepdims=True)
    coarse_z = 0.5 * expand(both)
    z = exchange_end(0) + coarse_z

    prod = product(z, ah_ref, al_ref)
    exchange_start(1, prod)
    dp = sums_of(z, prod)
    gx_begin(0, jnp.where(sub == 0, rz, dp))
    image = exchange_end(1)

    half = 0.5 * image
    mean_q = averages(half)
    avg_begin(1, mean_q)
    z_begin(0, gx_total(0))
    local_q = 0.5 * product(half, xh_ref, xl_ref)
    exchange_start(2, local_q)
    own_q, both_q = amounts(1)
    coarse_q = 0.5 * expand(both_q)
    q = exchange_end(2) + coarse_q
    first = z_total(0)
    valid = lax.broadcasted_iota(jnp.int32, (1, BW), 1) < R
    rz0 = first[0:1]
    dp0 = first[1:2]
    alpha0 = rz0 / jnp.where(valid, dp0, 1.0)
    alpha0_rows = per_row(alpha0)
    z1 = z - alpha0_rows * q

    prod1 = product(z1, ah_ref, al_ref)
    exchange_start(3, prod1)
    residual = right_side - alpha0_rows * image
    rz = sums_of(residual, local_z - alpha0_rows * local_q) + ROOT * jnp.sum(
        (own - alpha0 * own_q) * (mean - alpha0 * mean_q), axis=0, keepdims=True
    )
    zz = sums_of(z1, prod1)
    zd = sums_of(z1, prod)
    gx_begin(1, jnp.where(sub == 0, rz, jnp.where(sub == 1, zz, zd)))
    z_begin(1, gx_total(1))
    image1 = exchange_end(3)
    last = z_total(1)
    rz1 = last[0:1]
    beta = rz1 / jnp.where(valid, rz0, 1.0)
    energy = last[1:2] + 2.0 * beta * last[2:3] + beta * beta * dp0
    alpha1 = rz1 / jnp.where(valid, energy, 1.0)
    alpha1_rows = per_row(alpha1)
    beta_rows = per_row(beta)
    sol_ref[...] = alpha0_rows * z + alpha1_rows * (z1 + beta_rows * z)
    res_ref[...] = residual - alpha1_rows * (image1 + beta_rows * image)
    for copy in started:
        copy.wait_send()


def iterate(n_grp, n_sub, *args):
    n_z = n_sub // X_DIM
    n_gx = n_grp * X_DIM
    out = jax.ShapeDtypeStruct((R, M), F32)
    dma = pltpu.SemaphoreType.DMA
    return pl.pallas_call(
        iterate_kernel,
        out_shape=(out, out),
        in_specs=[vmem()] * len(args),
        out_specs=(vmem(), vmem()),
        scratch_shapes=[
            pltpu.VMEM((M, M), BF16),
            pltpu.VMEM((M, M), BF16),
            pltpu.VMEM((M, M), F32),
            pltpu.VMEM((M, 4 * BW), BF16),
            pltpu.VMEM((4 * BW, M), BF16),
            pltpu.VMEM((BW, M), F32),
            pltpu.VMEM((BW, BW), F32),
            pltpu.VMEM((BW, BW), F32),
            pltpu.VMEM((5, 2, R, M // 2), F32),
            pltpu.VMEM((5, 2, R, M // 2), F32),
            pltpu.VMEM((n_grp, 8, BW), F32),
            pltpu.VMEM((2, 3, n_grp, 8, BW), F32),
            pltpu.VMEM((8, BW), F32),
            pltpu.VMEM((2, 8, BW), F32),
            pltpu.VMEM((2, n_gx, 8, BW), F32),
            pltpu.VMEM((2, n_z, 8, BW), F32),
            dma((5, 2)),
            dma((5, 2)),
            dma((n_grp,)),
            dma((n_grp,)),
            dma((2, 3, n_grp)),
            dma((2, 3, n_grp)),
            dma((2,)),
            dma((2,)),
            dma((2, n_gx)),
            dma((2, n_gx)),
            dma((2, n_z)),
            dma((2, n_z)),
        ],
        compiler_params=pltpu.CompilerParams(
            collective_id=0, has_side_effects=True, vmem_limit_bytes=40 * MIB
        ),
        cost_estimate=pl.CostEstimate(
            flops=2_000_000_000, bytes_accessed=10 * MIB, transcendentals=0
        ),
        name="iterate",
    )(*args)


def body(schur, loads, block_map, primal_map, disk_mask):
    a_high, a_low, x, inv, pivot, face, tile = invert(
        block_map[0], primal_map[0], schur[0, 0], loads[0, 0], disk_mask[0]
    )
    sol, res = iterate(
        lax.axis_size("grp"), lax.axis_size("sub"), face, tile, a_high, a_low, x, inv, pivot
    )
    return sol[None, None], res[None, None]


def solution(mesh):
    in_specs = (
        P("sub", "grp", None, None),
        P("sub", "grp", None, None),
        P("sub", "grp", None),
        P("sub", "grp", None),
        P("sub", "grp", None),
    )
    out_specs = (P("sub", "grp", None, None), P("sub", "grp", None, None))
    return jax.shard_map(body, mesh=mesh, in_specs=in_specs, out_specs=out_specs, check_vma=False)
```
